32 devices in a mesh: blk: 32 (over z, y, x, core).
Axes of the slice: x: 2, y: 2, z: 4, core: 2. Of those that a mesh axis runs over, the one named last changes fastest.
Arguments:
- query_states: bfloat16 [8192, 4096], P('blk'), may hold values from -6 to 6
- rotated_key_state: bfloat16 [8192, 1024], P('blk'), may hold values from -6 to 6
- value_state_rows: bfloat16 [8192, 1024], P('blk'), may hold values from -6 to 6
- positions: int32 [8192], P('blk'), may hold values from 0 to 1535, as said below
- residual: bfloat16 [8192, 4096], P('blk'), may hold values from -6 to 6
- norm_gain: float32 [4096], replicated, may hold values from 0.1 to 1.9
- gate_weight: bfloat16 [14336, 4096], P('blk'), may hold values from -0.09375 to 0.09375
- up_weight: bfloat16 [14336, 4096], P('blk'), may hold values from -0.09375 to 0.09375
- down_weight: bfloat16 [14336, 4096], P('blk'), may hold values from -0.125 to 0.125
Outputs:
- attended: bfloat16 [8192, 4096], P('blk')
- ffn_part: bfloat16 [8192, 4096], P('blk')
The draws below stay inside these ranges and needn't reach their ends.
Inputs may be any that keep to these rules, and one draw needn't show every extreme that they name: positions[0] is 0 and every later entry is 0 or one more than the entry before it.
All inputs are finite; a program needn't handle non-finite values.
Results may differ from the reference program's by a relative error of at most 0.0065.
Values may be sent and summed in bfloat16 or wider, within the bound.
A program may use at most 128 MiB of HBM per device.

```python
import math
import jax
import jax.numpy as jnp
from jax import lax

D = 4096
FF = 14336
QUERY_HEADS = 32
KEY_VALUE_HEADS = 8
HEAD_SIZE = 128
BLOCK_TOKENS = 256
WINDOW_BLOCKS = 4
FFN_STEPS = 4
SEQUENCE_TOKENS = 8192
DOC_MOST = 1536
N_BLK = 32


def random_noise(key, shape):
    return jnp.clip(jax.random.normal(key, shape, jnp.float32), -6.0, 6.0)


def draw_query_states(key, part):
    base_offset = random_noise(jax.random.fold_in(key, 1), (SEQUENCE_TOKENS, QUERY_HEADS * HEAD_SIZE))
    return base_offset.astype(jnp.bfloat16)


def draw_rotated_key_state(key, part):
    base_offset = random_noise(jax.random.fold_in(key, 2), (SEQUENCE_TOKENS, KEY_VALUE_HEADS * HEAD_SIZE))
    return base_offset.astype(jnp.bfloat16)


def draw_positions(key, part):
    number_blocks = SEQUENCE_TOKENS // BLOCK_TOKENS
    doc_count = 2 * number_blocks + 2
    first_key, another_key = jax.random.split(jax.random.fold_in(key, 3))
    lengths = jax.random.randint(first_key, (doc_count,), BLOCK_TOKENS // 2, DOC_MOST + 1)
    longest = jax.random.randint(another_key, (), 0, SEQUENCE_TOKENS // DOC_MOST)
    lengths = jnp.where(jnp.arange(doc_count) == longest, DOC_MOST, lengths)
    starts = jnp.cumsum(lengths) - lengths
    start_flags = jnp.zeros((SEQUENCE_TOKENS,), jnp.int32).at[starts].set(1, mode='drop')
    indices = jnp.arange(SEQUENCE_TOKENS, dtype=jnp.int32)
    doc_begin = lax.cummax(jnp.where(start_flags > 0, indices, 0), axis=0)
    return (indices - doc_begin).astype(jnp.int32)


def steps_of(own_key, dims, shards, least, largest):
    def one(axis_at, shards_of):
        steps = jax.random.uniform(jax.random.fold_in(jax.random.fold_in(own_key, 6), axis_at), (shards_of,), jnp.float32, least / len(shards), largest / len(shards))
        return jnp.repeat(jnp.exp(steps), dims[axis_at] // shards_of).reshape((-1,) + (1,) * (len(dims) - axis_at - 1))

    factor_of = one(*shards[0])
    for cut in shards[1:]:
        factor_of = factor_of * one(*cut)
    return factor_of


def noise(key, dims, width, reach, cuts=(), kind=jnp.bfloat16):
    drawn = jax.random.normal(key, dims, jnp.float32) * width
    if len(cuts) > 0:
        drawn = steps_of(key, dims, cuts, -0.22, 0.18) * drawn
    return jnp.clip(drawn, min=-reach, max=reach).astype(kind)


def setup_inputs(seed: int = 0) -> dict:
    splits = jax.random.split(jax.random.key(seed), 10)
    query_states = draw_query_states(jax.random.fold_in(splits[9], 71), 0)
    rotated_key_state = draw_rotated_key_state(jax.random.fold_in(splits[9], 71), 0)
    value_state_rows = noise(splits[2], (SEQUENCE_TOKENS, KEY_VALUE_HEADS * HEAD_SIZE), 1.0, 6.0, ((0, 32),))
    positions = draw_positions(jax.random.fold_in(splits[9], 71), 0)
    residual = noise(splits[4], (SEQUENCE_TOKENS, D), 1.0, 6.0, ((0, 32),))
    norm_gain = jnp.clip(1.0 + 0.18 * jax.random.normal(splits[5], (D,), jnp.float32), 0.1, 1.9)
    gate_weight = noise(splits[6], (FF, D), D ** -0.5, 0.09375, ((0, 32),))
    up_weight = noise(splits[7], (FF, D), D ** -0.5, 0.09375, ((0, 32),))
    down_weight = noise(splits[8], (FF, D), (FFN_STEPS * FF // N_BLK) ** -0.5, 0.125, ((0, 32),))
    return dict(query_states=query_states, rotated_key_state=rotated_key_state, value_state_rows=value_state_rows, positions=positions, residual=residual, norm_gain=norm_gain, gate_weight=gate_weight, up_weight=up_weight, down_weight=down_weight)


def reference(query_states, rotated_key_state, value_state_rows, positions, residual, norm_gain, gate_weight, up_weight, down_weight):
    number_blocks = SEQUENCE_TOKENS // BLOCK_TOKENS
    heads_per_group = QUERY_HEADS // KEY_VALUE_HEADS
    shard_rows = FF // number_blocks
    padding_rows = (WINDOW_BLOCKS - 1) * BLOCK_TOKENS
    key_with_padding = jnp.concatenate([jnp.zeros((padding_rows, KEY_VALUE_HEADS * HEAD_SIZE), rotated_key_state.dtype), rotated_key_state], axis=0)
    value_with_padding = jnp.concatenate([jnp.zeros((padding_rows, KEY_VALUE_HEADS * HEAD_SIZE), value_state_rows.dtype), value_state_rows], axis=0)
    gate_shards = gate_weight.reshape(number_blocks, shard_rows, D)
    up_shards = up_weight.reshape(number_blocks, shard_rows, D)
    down_shards = down_weight.reshape(number_blocks, shard_rows, D)
    score_scale = 1.0 / math.sqrt(HEAD_SIZE)
    contract = (((1,), (1,)), ((), ()))

    def one_block(block_index):
        start = (block_index * BLOCK_TOKENS).astype(jnp.int32)
        local_queries = lax.dynamic_slice_in_dim(query_states, start, BLOCK_TOKENS, 0)
        local_keys = lax.dynamic_slice_in_dim(key_with_padding, start, WINDOW_BLOCKS * BLOCK_TOKENS, 0)
        local_values = lax.dynamic_slice_in_dim(value_with_padding, start, WINDOW_BLOCKS * BLOCK_TOKENS, 0)
        positions_here = lax.dynamic_slice_in_dim(positions, start, BLOCK_TOKENS, 0)
        residual_here = lax.dynamic_slice_in_dim(residual, start, BLOCK_TOKENS, 0)
        query_index = start + jnp.arange(BLOCK_TOKENS, dtype=jnp.int32)
        key_index = start - padding_rows + jnp.arange(WINDOW_BLOCKS * BLOCK_TOKENS, dtype=jnp.int32)
        visible = (key_index[None, :] <= query_index[:, None]) & (key_index[None, :] >= (query_index - positions_here)[:, None])
        query_wide_float = local_queries.astype(jnp.float32).reshape(BLOCK_TOKENS, KEY_VALUE_HEADS, heads_per_group, HEAD_SIZE)
        key_wide_float = local_keys.astype(jnp.float32).reshape(WINDOW_BLOCKS * BLOCK_TOKENS, KEY_VALUE_HEADS, HEAD_SIZE)
        value_wide_float = local_values.astype(jnp.float32).reshape(WINDOW_BLOCKS * BLOCK_TOKENS, KEY_VALUE_HEADS, HEAD_SIZE)
        scores = jnp.einsum('tgrd,kgd->grtk', query_wide_float, key_wide_float) * score_scale
        scores = jnp.where(visible[None, None], scores, -jnp.inf)
        row_max = lax.optimization_barrier(jnp.max(scores, axis=-1, keepdims=True))
        weights = jnp.exp(scores - row_max)
        denominator = lax.optimization_barrier(jnp.sum(weights, axis=-1, keepdims=True))
        weights_rounded = lax.optimization_barrier(weights.astype(jnp.bfloat16)).astype(jnp.float32)
        mixed = jnp.einsum('grtk,kgd->grtd', weights_rounded, value_wide_float) / denominator
        attended = jnp.transpose(mixed, (2, 0, 1, 3)).reshape(BLOCK_TOKENS, QUERY_HEADS * HEAD_SIZE).astype(jnp.bfloat16)
        stream = residual_here.astype(jnp.float32) + attended.astype(jnp.float32)
        normed = (stream * lax.rsqrt(lax.optimization_barrier(jnp.mean(stream * stream, axis=-1, keepdims=True)) + 1e-05) * norm_gain).astype(jnp.bfloat16)
        owners = (block_index + jnp.arange(FFN_STEPS, dtype=jnp.int32)) % number_blocks
        gate_rows = jnp.take(gate_shards, owners, axis=0).reshape(FFN_STEPS * shard_rows, D)
        up_rows = jnp.take(up_shards, owners, axis=0).reshape(FFN_STEPS * shard_rows, D)
        down_rows = jnp.take(down_shards, owners, axis=0).reshape(FFN_STEPS * shard_rows, D)
        gate_value = lax.dot_general(normed, gate_rows, contract, preferred_element_type=jnp.float32)
        up_value = lax.dot_general(normed, up_rows, contract, preferred_element_type=jnp.float32)
        hidden = (jax.nn.silu(gate_value) * up_value).astype(jnp.bfloat16)
        ffn_part = jnp.dot(hidden, down_rows, preferred_element_type=jnp.float32).astype(jnp.bfloat16)
        return (attended, ffn_part)
    attended_all, ffn_all = lax.map(one_block, jnp.arange(number_blocks, dtype=jnp.int32))
    return (attended_all.reshape(SEQUENCE_TOKENS, QUERY_HEADS * HEAD_SIZE), ffn_all.reshape(SEQUENCE_TOKENS, D))
```

```python
import math

import jax
import jax.numpy as jnp
from jax import lax
from jax.sharding import PartitionSpec as P

QUERY_HEADS = 32
KEY_VALUE_HEADS = 8
HEAD_SIZE = 128
WINDOW_BLOCKS = 4
FFN_STEPS = 4


def passed_along(value, axis, by):
    length = lax.axis_size(axis)
    pairs = [(i, i + by) for i in range(length) if 0 <= i + by < length]
    return lax.ppermute(value, axis, pairs)


def shifted(value, axis, steps):
    count = lax.axis_size(axis)
    pairs = [(source, (source + steps) % count) for source in range(count)]
    return lax.ppermute(value, axis, pairs)


def shard_term(rows_in, gate_rows, up_rows, down_rows):
    contract = (((1,), (1,)), ((), ()))
    gate_value = lax.dot_general(rows_in, gate_rows, contract, preferred_element_type=jnp.float32)
    up_value = lax.dot_general(rows_in, up_rows, contract, preferred_element_type=jnp.float32)
    hidden = (jax.nn.silu(gate_value) * up_value).astype(jnp.bfloat16)
    return jnp.dot(hidden, down_rows, preferred_element_type=jnp.float32)


def per_device(
    query_states,
    rotated_key_state,
    value_state_rows,
    positions,
    residual,
    norm_gain,
    gate_weight,
    up_weight,
    down_weight,
):
    block_rows = query_states.shape[0]
    device_index = lax.axis_index("blk")
    heads_per_group = QUERY_HEADS // KEY_VALUE_HEADS
    arrived = [(rotated_key_state, value_state_rows)]
    for offset in range(1, WINDOW_BLOCKS):
        arrived.append(passed_along((rotated_key_state, value_state_rows), "blk", offset))
    ordered = arrived[::-1]
    key_window = jnp.concatenate([block_pair[0] for block_pair in ordered], axis=0)
    value_window = jnp.concatenate([block_pair[1] for block_pair in ordered], axis=0)
    query_index = device_index * block_rows + jnp.arange(block_rows, dtype=jnp.int32)
    key_index = (device_index - (WINDOW_BLOCKS - 1)) * block_rows + jnp.arange(
        WINDOW_BLOCKS * block_rows, dtype=jnp.int32
    )
    visible = (key_index[None, :] <= query_index[:, None]) & (
        key_index[None, :] >= (query_index - positions)[:, None]
    )
    score_scale = 1.0 / math.sqrt(HEAD_SIZE)

    def group_of_head(group_index, attended_rows):
        query_block = lax.dynamic_slice_in_dim(
            query_states, group_index * heads_per_group * HEAD_SIZE, heads_per_group * HEAD_SIZE, 1
        )
        query_block = query_block.reshape(block_rows, heads_per_group, HEAD_SIZE)
        key_block = lax.dynamic_slice_in_dim(key_window, group_index * HEAD_SIZE, HEAD_SIZE, 1)
        value_block = lax.dynamic_slice_in_dim(value_window, group_index * HEAD_SIZE, HEAD_SIZE, 1)
        scores = (
            jnp.einsum("trd,kd->rtk", query_block, key_block, preferred_element_type=jnp.float32)
            * score_scale
        )
        scores = jnp.where(visible[None], scores, -jnp.inf)
        row_max = jnp.max(scores, axis=-1, keepdims=True)
        weights = jnp.exp(scores - row_max)
        denominator = jnp.sum(weights, axis=-1, keepdims=True)
        mixed = (
            jnp.einsum(
                "rtk,kd->rtd",
                weights.astype(jnp.bfloat16),
                value_block,
                preferred_element_type=jnp.float32,
            )
            / denominator
        )
        result = (
            jnp.transpose(mixed, (1, 0, 2))
            .reshape(block_rows, heads_per_group * HEAD_SIZE)
            .astype(jnp.bfloat16)
        )
        return lax.dynamic_update_slice_in_dim(
            attended_rows, result, group_index * heads_per_group * HEAD_SIZE, 1
        )

    attended = lax.fori_loop(
        0,
        KEY_VALUE_HEADS,
        group_of_head,
        jnp.zeros((block_rows, QUERY_HEADS * HEAD_SIZE), jnp.bfloat16),
    )
    stream = residual.astype(jnp.float32) + attended.astype(jnp.float32)
    normed = (
        stream * lax.rsqrt(jnp.mean(stream * stream, axis=-1, keepdims=True) + 1e-05) * norm_gain
    ).astype(jnp.bfloat16)
    met = [normed] + [shifted(normed, "blk", offset) for offset in range(1, FFN_STEPS)]
    ffn_total = shard_term(met[0], gate_weight, up_weight, down_weight)
    parts = []
    for offset in range(1, FFN_STEPS):
        part = shard_term(met[offset], gate_weight, up_weight, down_weight).astype(jnp.bfloat16)
        parts.append(shifted(part, "blk", -offset))
    for part in parts:
        ffn_total = ffn_total + part.astype(jnp.float32)
    return (attended, ffn_total.astype(jnp.bfloat16))


def solution(mesh):
    in_specs = (
        P("blk", None),
        P("blk", None),
        P("blk", None),
        P("blk"),
        P("blk", None),
        P(),
        P("blk", None),
        P("blk", None),
        P("blk", None),
    )
    out_specs = (P("blk", None), P("blk", None))
    return jax.shard_map(
        per_device, mesh=mesh, in_specs=in_specs, out_specs=out_specs, check_vma=False
    )
```

```python
import functools
import math

import jax
import jax.numpy as jnp
from jax import lax
from jax.experimental import pallas as pl
from jax.experimental.pallas import tpu as pltpu
from jax.sharding import PartitionSpec as P

HEAD_SIZE = 128
KEY_VALUE_HEADS = 8
HEADS_PER_GROUP = 4
WINDOW_BLOCKS = 4
FFN_STEPS = 4
CHUNK = HEADS_PER_GROUP * HEAD_SIZE
PAIR = 2 * HEAD_SIZE
MESH = pl.DeviceIdType.MESH
NT = (((1,), (1,)), ((), ()))


def layer_kernel(
    count,
    q_hbm,
    k_hbm,
    v_hbm,
    pos_ref,
    res_hbm,
    gain_ref,
    gate_hbm,
    up_hbm,
    down_hbm,
    attended_hbm,
    ffn_hbm,
    q,
    k_own,
    v_own,
    res,
    gate,
    up,
    down,
    k_in,
    v_in,
    bias,
    s_own,
    s_in,
    square,
    rs_own,
    rs_in,
    acc_gate,
    acc_up,
    hidden,
    part,
    x_in,
    r_in,
    att,
    ffn,
    load_sem,
    att_sem,
    ffn_sem,
    kv_send,
    kv_recv,
    s_send,
    s_recv,
    rs_send,
    rs_recv,
    p_send,
    p_recv,
):
    rows, width = q.shape
    groups = KEY_VALUE_HEADS
    pairs = groups // 2
    me = lax.axis_index("blk")
    core = lax.rem(me, 2)

    def at(offset):
        return lax.rem(me + offset + count, count)

    two_on = at(2)
    third, third_slot = at(1 + 2 * core), 2 * core
    sibling, sibling_slot = at(1 - 2 * core), 2 - 2 * core
    routes = ((two_on, 1), (third, third_slot), (sibling, sibling_slot))

    loads = [
        pltpu.make_async_copy(src, dst, load_sem.at[i])
        for i, (src, dst) in enumerate(
            (
                (k_hbm, k_own),
                (v_hbm, v_own),
                (q_hbm, q),
                (res_hbm, res),
                (gate_hbm, gate),
                (up_hbm, up),
                (down_hbm, down),
            )
        )
    ]
    for load in loads:
        load.start()

    barrier = pltpu.get_barrier_semaphore()
    for offset in (1, 2, 3, -1, -2, -3):
        pl.semaphore_signal(barrier, inc=1, device_id=(at(offset),), device_id_type=MESH)
    pl.semaphore_wait(barrier, 6)

    def kv_copy(which, route, j):
        device, slot = routes[route]
        own, arrived = ((k_hbm, k_in), (v_hbm, v_in))[which]
        if route == 2:
            src = arrived.at[1, j]
        else:
            src = own.at[:, pl.ds(pl.multiple_of(j * PAIR, PAIR), PAIR)]
        return pltpu.make_async_remote_copy(
            src_ref=src,
            dst_ref=arrived.at[slot, j],
            send_sem=kv_send.at[which, route, j],
            recv_sem=kv_recv.at[which, slot, j],
            device_id=(device,),
            device_id_type=MESH,
        )

    def kv_arrival(which, slot, j):
        arrived = (k_in, v_in)[which]
        pltpu.make_async_copy(arrived.at[slot, j], arrived.at[slot, j], kv_recv.at[which, slot, j]).wait()

    def s_copy(route, g):
        device, slot = routes[route]
        return pltpu.make_async_remote_copy(
            src_ref=s_in.at[1, g] if route == 2 else s_own.at[g],
            dst_ref=s_in.at[slot, g],
            send_sem=s_send.at[route, g],
            recv_sem=s_recv.at[slot, g],
            device_id=(device,),
            device_id_type=MESH,
        )

    def s_arrival(slot, g):
        pltpu.make_async_copy(s_in.at[slot, g], s_in.at[slot, g], s_recv.at[slot, g]).wait()

    def rs_copy(route):
        device, slot = routes[route]
        return pltpu.make_async_remote_copy(
            src_ref=rs_in.at[1] if route == 2 else rs_own,
            dst_ref=rs_in.at[slot],
            send_sem=rs_send.at[route],
            recv_sem=rs_recv.at[slot],
            device_id=(device,),
            device_id_type=MESH,
        )

    def rs_arrival(slot):
        pltpu.make_async_copy(rs_in.at[slot], rs_in.at[slot], rs_recv.at[slot]).wait()

    def p_copy(kind, g):
        device = (sibling, at(-2), at(2 * core - 3))[kind]
        dst = x_in.at[g] if kind == 0 else r_in.at[kind - 1, g]
        return pltpu.make_async_remote_copy(
            src_ref=part.at[kind, g],
            dst_ref=dst,
            send_sem=p_send.at[kind, g],
            recv_sem=p_recv.at[kind, g],
            device_id=(device,),
            device_id_type=MESH,
        )

    def p_arrival(kind, g):
        dst = x_in.at[g] if kind == 0 else r_in.at[kind - 1, g]
        pltpu.make_async_copy(dst, dst, p_recv.at[kind, g]).wait()

    def each(limit):
        def run(body):
            lax.fori_loop(0, limit, lambda i, c: (body(i), c)[1], 0)

        return run

    @each(pairs)
    def _(j):
        for which in range(2):
            for route in range(2):
                kv_copy(which, route, j).start()

    row = lax.broadcasted_iota(jnp.int32, (rows, rows), 0)
    column = lax.broadcasted_iota(jnp.int32, (rows, rows), 1)
    for d in range(WINDOW_BLOCKS):
        key = column - d * rows
        seen = (key <= row) & (key >= row - pos_ref[...])
        bias[d] = jnp.where(seen, 0.0, -jnp.inf)
    square[...] = jnp.zeros_like(square)
    for load in loads[:4]:
        load.wait()

    factor = math.log2(math.e) / math.sqrt(HEAD_SIZE)

    @each(pairs)
    def _(j):
        for which in range(2):
            kv_arrival(which, 1, j)
            kv_copy(which, 2, j).start()
        for which in range(2):
            kv_arrival(which, 0, j)
            kv_arrival(which, 2, j)
        for half in range(2):
            g = 2 * j + half
            here = pl.ds(half * HEAD_SIZE, HEAD_SIZE)
            kv_cols = pl.ds(pl.multiple_of(g * HEAD_SIZE, HEAD_SIZE), HEAD_SIZE)
            keys = [k_own[:, kv_cols]] + [k_in[s, j, :, here] for s in range(3)]
            values = [v_own[:, kv_cols]] + [v_in[s, j, :, here] for s in range(3)]
            for h in range(HEADS_PER_GROUP):
                cols = pl.ds(pl.multiple_of(g * CHUNK + h * HEAD_SIZE, HEAD_SIZE), HEAD_SIZE)
                inner = pl.ds(h * HEAD_SIZE, HEAD_SIZE)
                query = q[:, cols]
                scores = [
                    lax.dot_general(query, keys[d], NT, preferred_element_type=jnp.float32) + bias[d]
                    for d in range(WINDOW_BLOCKS)
                ]
                top = functools.reduce(jnp.maximum, scores)
                top = jnp.max(top, axis=1, keepdims=True)
                weights = [jnp.exp2((score - top) * factor) for score in scores]
                total = jnp.sum(functools.reduce(jnp.add, weights), axis=1, keepdims=True)
                mixed = functools.reduce(
                    jnp.add,
                    [
                        jnp.dot(w.astype(jnp.bfloat16), v, preferred_element_type=jnp.float32)
                        for w, v in zip(weights, values)
                    ],
                )
                attended = (mixed / total).astype(jnp.bfloat16)
                att[:, cols] = attended
                stream = res[:, cols].astype(jnp.float32) + attended.astype(jnp.float32)
                square[...] += stream * stream
                s_own[g, :, inner] = (stream * gain_ref[:, cols]).astype(jnp.bfloat16)
            s_copy(0, g).start()
            s_copy(1, g).start()

    att_copy = pltpu.make_async_copy(att, attended_hbm, att_sem)
    att_copy.start()
    mean = jnp.sum(square[...], axis=1, keepdims=True) * (1.0 / width)
    rs_own[...] = jnp.broadcast_to(lax.rsqrt(mean + 1e-05), rs_own.shape)
    rs_copy(0).start()
    rs_copy(1).start()
    for load in loads[4:]:
        load.wait()
    acc_gate[...] = jnp.zeros_like(acc_gate)
    acc_up[...] = jnp.zeros_like(acc_up)

    def add_chunk(place, chunk, g):
        cols = pl.ds(pl.multiple_of(g * CHUNK, CHUNK), CHUNK)
        acc_gate[place] += lax.dot_general(chunk, gate[:, cols], NT, preferred_element_type=jnp.float32)
        acc_up[place] += lax.dot_general(chunk, up[:, cols], NT, preferred_element_type=jnp.float32)

    def make_hidden(place, scale):
        gate_value = acc_gate[place] * scale[:, :1]
        up_value = acc_up[place] * scale[:, :1]
        silu = gate_value / (1.0 + jnp.exp(-gate_value))
        hidden[place] = (silu * up_value).astype(jnp.bfloat16)

    def down_chunk(place, g):
        cols = pl.ds(pl.multiple_of(g * CHUNK, CHUNK), CHUNK)
        return jnp.dot(hidden[place], down[:, cols], preferred_element_type=jnp.float32)

    @each(groups)
    def _(g):
        s_arrival(1, g)
        s_copy(2, g).start()
        add_chunk(3, s_own[g], g)
        add_chunk(1, s_in[1, g], g)

    rs_arrival(1)
    rs_copy(2).start()
    make_hidden(3, rs_own[...])
    make_hidden(1, rs_in[1])

    @each(groups)
    def _(g):
        s_arrival(2 - 2 * core, g)
        add_chunk(2, s_in[2 - 2 * core, g], g)

    rs_arrival(2 - 2 * core)
    make_hidden(2, rs_in[2 - 2 * core])

    @each(groups)
    def _(g):
        part[2, g] = down_chunk(2, g).astype(jnp.bfloat16)
        p_copy(2, g).start()

    @each(groups)
    def _(g):
        s_arrival(2 * core, g)
        add_chunk(0, s_in[2 * core, g], g)

    rs_arrival(2 * core)
    make_hidden(0, rs_in[2 * core])

    @each(groups)
    def _(g):
        part[0, g] = down_chunk(0, g).astype(jnp.bfloat16)
        p_copy(0, g).start()

    @each(groups)
    def _(g):
        mine = down_chunk(1, g)
        p_arrival(0, g)
        part[1, g] = (mine + x_in[g].astype(jnp.float32)).astype(jnp.bfloat16)
        p_copy(1, g).start()

    @each(groups)
    def _(g):
        cols = pl.ds(pl.multiple_of(g * CHUNK, CHUNK), CHUNK)
        mine = down_chunk(3, g)
        p_arrival(2, g)
        p_arrival(1, g)
        total = mine + r_in[0, g].astype(jnp.float32) + r_in[1, g].astype(jnp.float32)
        ffn[:, cols] = total.astype(jnp.bfloat16)

    ffn_copy = pltpu.make_async_copy(ffn, ffn_hbm, ffn_sem)
    ffn_copy.start()

    @each(pairs)
    def _(j):
        for which in range(2):
            for route in range(3):
                kv_copy(which, route, j).wait_send()

    @each(groups)
    def _(g):
        for route in range(3):
            s_copy(route, g).wait_send()
            p_copy(route, g).wait_send()

    for route in range(3):
        rs_copy(route).wait_send()
    att_copy.wait()
    ffn_copy.wait()


def per_device(count, q, k, v, positions, residual, gain, gate, up, down):
    rows, width = q.shape
    units = gate.shape[0]
    groups = KEY_VALUE_HEADS
    pairs = groups // 2
    bf16, f32 = jnp.bfloat16, jnp.float32
    any_spec = pl.BlockSpec(memory_space=pl.ANY)
    vmem_spec = pl.BlockSpec(memory_space=pltpu.VMEM)
    dma = pltpu.SemaphoreType.DMA
    return pl.pallas_call(
        functools.partial(layer_kernel, count),
        out_shape=(jax.ShapeDtypeStruct((rows, width), bf16),) * 2,
        in_specs=[any_spec, any_spec, any_spec, vmem_spec, any_spec, vmem_spec] + [any_spec] * 3,
        out_specs=(any_spec, any_spec),
        scratch_shapes=[
            pltpu.VMEM((rows, width), bf16),
            pltpu.VMEM(k.shape, bf16),
            pltpu.VMEM(v.shape, bf16),
            pltpu.VMEM((rows, width), bf16),
            pltpu.VMEM((units, width), bf16),
            pltpu.VMEM((units, width), bf16),
            pltpu.VMEM((units, width), bf16),
            pltpu.VMEM((3, pairs, rows, PAIR), bf16),
            pltpu.VMEM((3, pairs, rows, PAIR), bf16),
            pltpu.VMEM((WINDOW_BLOCKS, rows, rows), f32),
            pltpu.VMEM((groups, rows, CHUNK), bf16),
            pltpu.VMEM((3, groups, rows, CHUNK), bf16),
            pltpu.VMEM((rows, HEAD_SIZE), f32),
            pltpu.VMEM((rows, HEAD_SIZE), f32),
            pltpu.VMEM((3, rows, HEAD_SIZE), f32),
            pltpu.VMEM((FFN_STEPS, rows, units), f32),
            pltpu.VMEM((FFN_STEPS, rows, units), f32),
            pltpu.VMEM((FFN_STEPS, rows, units), bf16),
            pltpu.VMEM((3, groups, rows, CHUNK), bf16),
            pltpu.VMEM((groups, rows, CHUNK), bf16),
            pltpu.VMEM((2, groups, rows, CHUNK), bf16),
            pltpu.VMEM((rows, width), bf16),
            pltpu.VMEM((rows, width), bf16),
            dma((7,)),
            dma,
            dma,
            dma((2, 3, pairs)),
            dma((2, 3, pairs)),
            dma((3, groups)),
            dma((3, groups)),
            dma((3,)),
            dma((3,)),
            dma((3, groups)),
            dma((3, groups)),
        ],
        compiler_params=pltpu.CompilerParams(
            collective_id=0, has_side_effects=True, vmem_limit_bytes=60 * 2**20
        ),
    )(q, k, v, positions.reshape(rows, 1), residual, gain.reshape(1, width), gate, up, down)


def solution(mesh):
    split = P("blk", None)
    in_specs = (split, split, split, P("blk"), split, P(), split, split, split)
    return jax.shard_map(
        functools.partial(per_device, mesh.shape["blk"]),
        mesh=mesh,
        in_specs=in_specs,
        out_specs=(split, split),
        check_vma=False,
    )
```

```python
import functools
import math

import jax
import jax.numpy as jnp
from jax import lax
from jax.experimental import pallas as pl
from jax.experimental.pallas import tpu as pltpu
from jax.sharding import PartitionSpec as P

HEAD_SIZE = 128
KEY_VALUE_HEADS = 8
HEADS_PER_GROUP = 4
WINDOW_BLOCKS = 4
FFN_STEPS = 4
PAIR = 2 * HEAD_SIZE
CHUNK = HEADS_PER_GROUP * PAIR
TILES = 4
MESH = pl.DeviceIdType.MESH
NT = (((1,), (1,)), ((), ()))


def layer_kernel(
    count,
    q_hbm,
    k_hbm,
    v_hbm,
    pos_ref,
    res_hbm,
    gain_ref,
    gate_hbm,
    up_hbm,
    down_hbm,
    attended_hbm,
    ffn_hbm,
    q,
    k_own,
    v_own,
    res,
    gate,
    up,
    down,
    k_in,
    v_in,
    s_all,
    square,
    rs_all,
    acc_gate,
    acc_up,
    hidden,
    middle,
    own_total,
    part,
    x_in,
    r_in,
    att,
    ffn,
    load_sem,
    att_sem,
    ffn_sem,
    kv_send,
    kv_recv,
    s_send,
    s_recv,
    rs_send,
    rs_recv,
    p_send,
    p_recv,
):
    rows, width = q.shape
    pairs = KEY_VALUE_HEADS // 2
    tile = rows // TILES
    me = lax.axis_index("blk")
    core = lax.rem(me, 2)

    def at(offset):
        return lax.rem(me + offset + count, count)

    third, sibling = at(1 + 2 * core), at(1 - 2 * core)
    routes = ((at(2), 1, 0), (third, 2 * core, 2 + core), (sibling, 2 - 2 * core, 3 - core))

    loads = [
        pltpu.make_async_copy(src, dst, load_sem.at[i])
        for i, (src, dst) in enumerate(
            (
                (k_hbm, k_own),
                (v_hbm, v_own),
                (q_hbm, q),
                (res_hbm, res),
                (gate_hbm, gate),
                (up_hbm, up),
                (down_hbm, down),
            )
        )
    ]
    for load in loads:
        load.start()

    barrier = pltpu.get_barrier_semaphore()
    for offset in (1, 2, 3, -1, -2, -3):
        pl.semaphore_signal(barrier, inc=1, device_id=(at(offset),), device_id_type=MESH)
    pl.semaphore_wait(barrier, 6)

    def kv_copy(which, route, j):
        device, slot, _ = routes[route]
        own, arrived = ((k_hbm, k_in), (v_hbm, v_in))[which]
        if route == 2:
            src = arrived.at[1, j]
        else:
            src = own.at[:, pl.ds(pl.multiple_of(j * PAIR, PAIR), PAIR)]
        return pltpu.make_async_remote_copy(
            src_ref=src,
            dst_ref=arrived.at[slot, j],
            send_sem=kv_send.at[which, route, j],
            recv_sem=kv_recv.at[which, slot, j],
            device_id=(device,),
            device_id_type=MESH,
        )

    def kv_arrival(which, slot, j):
        arrived = (k_in, v_in)[which]
        pltpu.make_async_copy(arrived.at[slot, j], arrived.at[slot, j], kv_recv.at[which, slot, j]).wait()

    def s_copy(route, t, j):
        device, _, place = routes[route]
        return pltpu.make_async_remote_copy(
            src_ref=s_all.at[t, j, 0 if route == 2 else 1],
            dst_ref=s_all.at[t, j, place],
            send_sem=s_send.at[route, t, j],
            recv_sem=s_recv.at[place, t, j],
            device_id=(device,),
            device_id_type=MESH,
        )

    def s_arrival(place, t, j):
        here = s_all.at[t, j, place]
        pltpu.make_async_copy(here, here, s_recv.at[place, t, j]).wait()

    def rs_copy(route, t):
        device, _, place = routes[route]
        return pltpu.make_async_remote_copy(
            src_ref=rs_all.at[t, 0 if route == 2 else 1],
            dst_ref=rs_all.at[t, place],
            send_sem=rs_send.at[route, t],
            recv_sem=rs_recv.at[place, t],
            device_id=(device,),
            device_id_type=MESH,
        )

    def rs_arrival(place, t):
        here = rs_all.at[t, place]
        pltpu.make_async_copy(here, here, rs_recv.at[place, t]).wait()

    def p_landing(kind, t, j):
        return x_in.at[t, j] if kind == 0 else r_in.at[kind - 1, t, j]

    def p_copy(kind, t, j):
        return pltpu.make_async_remote_copy(
            src_ref=part.at[kind, t, j],
            dst_ref=p_landing(kind, t, j),
            send_sem=p_send.at[kind, t, j],
            recv_sem=p_recv.at[kind, t, j],
            device_id=((sibling, at(-2), at(2 * core - 3))[kind],),
            device_id_type=MESH,
        )

    def p_arrival(kind, t, j):
        here = p_landing(kind, t, j)
        pltpu.make_async_copy(here, here, p_recv.at[kind, t, j]).wait()

    def each(limit):
        def run(body):
            lax.fori_loop(0, limit, lambda i, c: (body(i), c)[1], 0)

        return run

    @each(pairs)
    def _(j):
        for which in range(2):
            for route in range(2):
                kv_copy(which, route, j).start()

    for load in loads[:4]:
        load.wait()

    factor = math.log2(math.e) / math.sqrt(HEAD_SIZE)
    row_ids = lax.broadcasted_iota(jnp.int32, (tile, rows), 0)
    column_ids = lax.broadcasted_iota(jnp.int32, (tile, rows), 1)

    def att_copy(t):
        here = pl.ds(pl.multiple_of(t * tile, tile), tile)
        return pltpu.make_async_copy(att.at[here], attended_hbm.at[here], att_sem.at[t])

    def ffn_copy(t):
        here = pl.ds(pl.multiple_of(t * tile, tile), tile)
        return pltpu.make_async_copy(ffn.at[here], ffn_hbm.at[here], ffn_sem.at[t])

    @each(TILES)
    def _(t):
        here = pl.ds(pl.multiple_of(t * tile, tile), tile)
        row = row_ids + t * tile
        first = row - pos_ref[here]
        bias = []
        for d in range(WINDOW_BLOCKS):
            key = column_ids - d * rows
            bias.append(jnp.where((key <= row) & (key >= first), 0.0, -jnp.inf))
        square[...] = jnp.zeros_like(square)

        @each(pairs)
        def _(j):
            @pl.when(t == 0)
            def _():
                for which in range(2):
                    kv_arrival(which, 1, j)
                    kv_copy(which, 2, j).start()
                for which in range(2):
                    kv_arrival(which, 0, j)
                    kv_arrival(which, 2, j)

            for half in range(2):
                inner = pl.ds(half * HEAD_SIZE, HEAD_SIZE)
                kv_cols = pl.ds(pl.multiple_of(j * PAIR + half * HEAD_SIZE, HEAD_SIZE), HEAD_SIZE)
                keys = [k_own[:, kv_cols]] + [k_in[s, j, :, inner] for s in range(3)]
                values = [v_own[:, kv_cols]] + [v_in[s, j, :, inner] for s in range(3)]
                starts = [(half * HEADS_PER_GROUP + h) * HEAD_SIZE for h in range(HEADS_PER_GROUP)]
                cols = [pl.ds(pl.multiple_of(j * CHUNK + at_, HEAD_SIZE), HEAD_SIZE) for at_ in starts]
                query = jnp.concatenate([q[here, c] for c in cols], axis=0)
                scores = []
                for d in range(WINDOW_BLOCKS):
                    score = lax.dot_general(query, keys[d], NT, preferred_element_type=jnp.float32)
                    score = score.reshape(HEADS_PER_GROUP, tile, rows) + bias[d][None]
                    scores.append(score.reshape(HEADS_PER_GROUP * tile, rows))
                top = functools.reduce(jnp.maximum, scores)
                top = jnp.max(top, axis=1, keepdims=True)
                weights = [jnp.exp2((score - top) * factor) for score in scores]
                total = jnp.sum(functools.reduce(jnp.add, weights), axis=1, keepdims=True)
                mixed = functools.reduce(
                    jnp.add,
                    [
                        jnp.dot(w.astype(jnp.bfloat16), v, preferred_element_type=jnp.float32)
                        for w, v in zip(weights, values)
                    ],
                )
                attended = (mixed / total).astype(jnp.bfloat16)
                for h in range(HEADS_PER_GROUP):
                    mine = attended[h * tile : (h + 1) * tile]
                    att[here, cols[h]] = mine
                    stream = res[here, cols[h]].astype(jnp.float32) + mine.astype(jnp.float32)
                    square[...] += stream * stream
                    s_all[t, j, 1, :, pl.ds(starts[h], HEAD_SIZE)] = (
                        stream * gain_ref[:, cols[h]]
                    ).astype(jnp.bfloat16)
            s_copy(0, t, j).start()
            s_copy(1, t, j).start()

        att_copy(t).start()
        mean = jnp.sum(square[...], axis=1, keepdims=True) * (1.0 / width)
        rs_all[t, 1] = jnp.broadcast_to(lax.rsqrt(mean + 1e-05), square.shape)
        rs_copy(0, t).start()
        rs_copy(1, t).start()

    for load in loads[4:]:
        load.wait()

    @each(TILES)
    def _(t):
        acc_gate[...] = jnp.zeros_like(acc_gate)
        acc_up[...] = jnp.zeros_like(acc_up)

        @each(pairs)
        def _(j):
            s_arrival(0, t, j)
            s_copy(2, t, j).start()

        rs_arrival(0, t)
        rs_copy(2, t).start()

        @each(pairs)
        def _(j):
            s_arrival(2, t, j)
            s_arrival(3, t, j)
            cols = pl.ds(pl.multiple_of(j * CHUNK, CHUNK), CHUNK)
            chunk = s_all[t, j].reshape(FFN_STEPS * tile, CHUNK)
            acc_gate[...] += lax.dot_general(chunk, gate[:, cols], NT, preferred_element_type=jnp.float32)
            acc_up[...] += lax.dot_general(chunk, up[:, cols], NT, preferred_element_type=jnp.float32)

        rs_arrival(2, t)
        rs_arrival(3, t)
        scale = rs_all[t].reshape(FFN_STEPS * tile, HEAD_SIZE)[:, :1]
        gate_value = acc_gate[...] * scale
        silu = gate_value / (1.0 + jnp.exp(-gate_value))
        hidden[...] = (silu * (acc_up[...] * scale)).astype(jnp.bfloat16).reshape(hidden.shape)

        @each(pairs)
        def _(j):
            cols = pl.ds(pl.multiple_of(j * CHUNK, CHUNK), CHUNK)
            fed = hidden[...].reshape(FFN_STEPS * tile, hidden.shape[2])
            sums = jnp.dot(fed, down[:, cols], preferred_element_type=jnp.float32)
            sums = sums.reshape(FFN_STEPS, tile, CHUNK)
            middle[j] = sums[0]
            own_total[t, j] = sums[1]
            even = core == 0
            part[0, t, j] = jnp.where(even, sums[2], sums[3]).astype(jnp.bfloat16)
            part[2, t, j] = jnp.where(even, sums[3], sums[2]).astype(jnp.bfloat16)
            p_copy(2, t, j).start()
            p_copy(0, t, j).start()

        @each(pairs)
        def _(j):
            p_arrival(0, t, j)
            part[1, t, j] = (middle[j] + x_in[t, j].astype(jnp.float32)).astype(jnp.bfloat16)
            p_copy(1, t, j).start()

    @each(TILES)
    def _(t):
        here = pl.ds(pl.multiple_of(t * tile, tile), tile)

        @each(pairs)
        def _(j):
            cols = pl.ds(pl.multiple_of(j * CHUNK, CHUNK), CHUNK)
            p_arrival(2, t, j)
            p_arrival(1, t, j)
            back = r_in[0, t, j].astype(jnp.float32) + r_in[1, t, j].astype(jnp.float32)
            ffn[here, cols] = (own_total[t, j] + back).astype(jnp.bfloat16)

        ffn_copy(t).start()

    @each(pairs)
    def _(j):
        for which in range(2):
            for route in range(3):
                kv_copy(which, route, j).wait_send()

    @each(TILES)
    def _(t):
        @each(pairs)
        def _(j):
            for route in range(3):
                s_copy(route, t, j).wait_send()
                p_copy(route, t, j).wait_send()

        for route in range(3):
            rs_copy(route, t).wait_send()
        att_copy(t).wait()
        ffn_copy(t).wait()


def per_device(count, q, k, v, positions, residual, gain, gate, up, down):
    rows, width = q.shape
    units = gate.shape[0]
    tile = rows // TILES
    pairs = KEY_VALUE_HEADS // 2
    bf16, f32 = jnp.bfloat16, jnp.float32
    any_spec = pl.BlockSpec(memory_space=pl.ANY)
    vmem_spec = pl.BlockSpec(memory_space=pltpu.VMEM)
    dma = pltpu.SemaphoreType.DMA
    return pl.pallas_call(
        functools.partial(layer_kernel, count),
        out_shape=(jax.ShapeDtypeStruct((rows, width), bf16),) * 2,
        in_specs=[any_spec, any_spec, any_spec, vmem_spec, any_spec, vmem_spec] + [any_spec] * 3,
        out_specs=(any_spec, any_spec),
        scratch_shapes=[
            pltpu.VMEM((rows, width), bf16),
            pltpu.VMEM(k.shape, bf16),
            pltpu.VMEM(v.shape, bf16),
            pltpu.VMEM((rows, width), bf16),
            pltpu.VMEM((units, width), bf16),
            pltpu.VMEM((units, width), bf16),
            pltpu.VMEM((units, width), bf16),
            pltpu.VMEM((3, pairs, rows, PAIR), bf16),
            pltpu.VMEM((3, pairs, rows, PAIR), bf16),
            pltpu.VMEM((TILES, pairs, FFN_STEPS, tile, CHUNK), bf16),
            pltpu.VMEM((tile, HEAD_SIZE), f32),
            pltpu.VMEM((TILES, FFN_STEPS, tile, HEAD_SIZE), f32),
            pltpu.VMEM((FFN_STEPS * tile, units), f32),
            pltpu.VMEM((FFN_STEPS * tile, units), f32),
            pltpu.VMEM((FFN_STEPS, tile, units), bf16),
            pltpu.VMEM((pairs, tile, CHUNK), f32),
            pltpu.VMEM((TILES, pairs, tile, CHUNK), f32),
            pltpu.VMEM((3, TILES, pairs, tile, CHUNK), bf16),
            pltpu.VMEM((TILES, pairs, tile, CHUNK), bf16),
            pltpu.VMEM((2, TILES, pairs, tile, CHUNK), bf16),
            pltpu.VMEM((rows, width), bf16),
            pltpu.VMEM((rows, width), bf16),
            dma((7,)),
            dma((TILES,)),
            dma((TILES,)),
            dma((2, 3, pairs)),
            dma((2, 3, pairs)),
            dma((3, TILES, pairs)),
            dma((4, TILES, pairs)),
            dma((3, TILES)),
            dma((4, TILES)),
            dma((3, TILES, pairs)),
            dma((3, TILES, pairs)),
        ],
        compiler_params=pltpu.CompilerParams(
            collective_id=0, has_side_effects=True, vmem_limit_bytes=60 * 2**20
        ),
    )(q, k, v, positions.reshape(rows, 1), residual, gain.reshape(1, width), gate, up, down)


def solution(mesh):
    split = P("blk", None)
    in_specs = (split, split, split, P("blk"), split, P(), split, split, split)
    return jax.shard_map(
        functools.partial(per_device, mesh.shape["blk"]),
        mesh=mesh,
        in_specs=in_specs,
        out_specs=(split, split),
        check_vma=False,
    )
```

```python
import functools
import math

import jax
import jax.numpy as jnp
from jax import lax
from jax.experimental import pallas as pl
from jax.experimental.pallas import tpu as pltpu
from jax.sharding import PartitionSpec as P

HEAD_SIZE = 128
KEY_VALUE_HEADS = 8
HEADS_PER_GROUP = 4
WINDOW_BLOCKS = 4
FFN_STEPS = 4
PAIR = 2 * HEAD_SIZE
CHUNK = HEADS_PER_GROUP * PAIR
TILES = 4
MESH = pl.DeviceIdType.MESH
NT = (((1,), (1,)), ((), ()))


def layer_kernel(
    count,
    q_hbm,
    k_hbm,
    v_hbm,
    pos_ref,
    res_hbm,
    gain_ref,
    gate_hbm,
    up_hbm,
    down_hbm,
    attended_hbm,
    ffn_hbm,
    q,
    k_own,
    v_own,
    res,
    gate,
    up,
    down,
    k_in,
    v_in,
    s_all,
    first_key,
    square,
    rs_all,
    acc_gate,
    acc_up,
    hidden,
    middle,
    own_total,
    part,
    x_in,
    r_in,
    att,
    ffn,
    load_sem,
    att_sem,
    ffn_sem,
    kv_send,
    kv_recv,
    s_send,
    s_recv,
    rs_send,
    rs_recv,
    p_send,
    p_recv,
):
    rows, width = q.shape
    pairs = KEY_VALUE_HEADS // 2
    tile = rows // TILES
    me = lax.axis_index("blk")
    core = lax.rem(me, 2)

    def at(offset):
        return lax.rem(me + offset + count, count)

    third, sibling = at(1 + 2 * core), at(1 - 2 * core)
    routes = ((at(2), 1, 0), (third, 2 * core, 2 + core), (sibling, 2 - 2 * core, 3 - core))

    loads = [
        pltpu.make_async_copy(src, dst, load_sem.at[i])
        for i, (src, dst) in enumerate(
            (
                (k_hbm, k_own),
                (v_hbm, v_own),
                (q_hbm, q),
                (res_hbm, res),
                (gate_hbm, gate),
                (up_hbm, up),
                (down_hbm, down),
            )
        )
    ]
    for load in loads:
        load.start()

    barrier = pltpu.get_barrier_semaphore()
    for offset in (1, 2, 3, -1, -2, -3):
        pl.semaphore_signal(barrier, inc=1, device_id=(at(offset),), device_id_type=MESH)
    pl.semaphore_wait(barrier, 6)

    def kv_copy(which, route, j):
        device, slot, _ = routes[route]
        own, arrived = ((k_hbm, k_in), (v_hbm, v_in))[which]
        if route == 2:
            src = arrived.at[1, j]
        else:
            src = own.at[:, pl.ds(pl.multiple_of(j * PAIR, PAIR), PAIR)]
        return pltpu.make_async_remote_copy(
            src_ref=src,
            dst_ref=arrived.at[slot, j],
            send_sem=kv_send.at[which, route, j],
            recv_sem=kv_recv.at[which, slot, j],
            device_id=(device,),
            device_id_type=MESH,
        )

    def kv_arrival(which, slot, j):
        arrived = (k_in, v_in)[which]
        pltpu.make_async_copy(arrived.at[slot, j], arrived.at[slot, j], kv_recv.at[which, slot, j]).wait()

    def s_copy(route, t, j):
        device, _, place = routes[route]
        return pltpu.make_async_remote_copy(
            src_ref=s_all.at[t, j, 0 if route == 2 else 1],
            dst_ref=s_all.at[t, j, place],
            send_sem=s_send.at[route, t, j],
            recv_sem=s_recv.at[place, t, j],
            device_id=(device,),
            device_id_type=MESH,
        )

    def s_arrival(place, t, j):
        here = s_all.at[t, j, place]
        pltpu.make_async_copy(here, here, s_recv.at[place, t, j]).wait()

    def rs_copy(route, t):
        device, _, place = routes[route]
        return pltpu.make_async_remote_copy(
            src_ref=rs_all.at[t, 0 if route == 2 else 1],
            dst_ref=rs_all.at[t, place],
            send_sem=rs_send.at[route, t],
            recv_sem=rs_recv.at[place, t],
            device_id=(device,),
            device_id_type=MESH,
        )

    def rs_arrival(place, t):
        here = rs_all.at[t, place]
        pltpu.make_async_copy(here, here, rs_recv.at[place, t]).wait()

    def p_landing(kind, t, j):
        return x_in.at[t, j] if kind == 0 else r_in.at[kind - 1, t, j]

    def p_copy(kind, t, j):
        return pltpu.make_async_remote_copy(
            src_ref=part.at[kind, t, j],
            dst_ref=p_landing(kind, t, j),
            send_sem=p_send.at[kind, t, j],
            recv_sem=p_recv.at[kind, t, j],
            device_id=((sibling, at(-2), at(2 * core - 3))[kind],),
            device_id_type=MESH,
        )

    def p_arrival(kind, t, j):
        here = p_landing(kind, t, j)
        pltpu.make_async_copy(here, here, p_recv.at[kind, t, j]).wait()

    def each(limit):
        def run(body):
            lax.fori_loop(0, limit, lambda i, c: (body(i), c)[1], 0)

        return run

    sends = (me + 2 < count, me + 1 + 2 * core < count)
    reaches = (me >= 1, me >= 2, me >= 3)
    forwards = reaches[1]

    def kv_each(route, act):
        @pl.when(forwards if route == 2 else sends[route])
        def _():
            @each(pairs)
            def _(j):
                for which in range(2):
                    act(kv_copy(which, route, j))

    for route in range(2):
        kv_each(route, lambda copy: copy.start())
    for slot in range(WINDOW_BLOCKS - 1):
        @pl.when(jnp.logical_not(reaches[slot]))
        def _():
            k_in[slot] = jnp.zeros(k_in.shape[1:], k_in.dtype)
            v_in[slot] = jnp.zeros(v_in.shape[1:], v_in.dtype)

    for load in loads[:4]:
        load.wait()

    factor = math.log2(math.e) / math.sqrt(HEAD_SIZE)
    row_ids = lax.broadcasted_iota(jnp.int32, (tile, rows), 0)
    column_ids = lax.broadcasted_iota(jnp.int32, (tile, rows), 1)

    def att_copy(t):
        here = pl.ds(pl.multiple_of(t * tile, tile), tile)
        return pltpu.make_async_copy(att.at[here], attended_hbm.at[here], att_sem.at[t])

    def ffn_copy(t):
        here = pl.ds(pl.multiple_of(t * tile, tile), tile)
        return pltpu.make_async_copy(ffn.at[here], ffn_hbm.at[here], ffn_sem.at[t])

    diagonal = lax.broadcasted_iota(jnp.int32, (rows, rows), 0) - lax.broadcasted_iota(
        jnp.int32, (rows, rows), 1
    )
    back = jnp.where(diagonal == 0, pos_ref[...].astype(jnp.float32), 0.0)
    first_key[...] = (
        lax.broadcasted_iota(jnp.int32, (rows, 1), 0).astype(jnp.float32)
        - jnp.sum(back, axis=1, keepdims=True)
    )
    square[...] = jnp.zeros_like(square)

    def send_rows(t, j):
        s_copy(0, t, j).start()
        s_copy(1, t, j).start()

    @each(pairs)
    def _(j):
        @pl.when(reaches[1])
        def _():
            for which in range(2):
                kv_arrival(which, 1, j)
                kv_copy(which, 2, j).start()

        for slot in (0, 2):
            @pl.when(reaches[slot])
            def _():
                for which in range(2):
                    kv_arrival(which, slot, j)

        @each(TILES)
        def _(t):
            here = pl.ds(pl.multiple_of(t * tile, tile), tile)
            row = row_ids + t * tile
            first = first_key[here]
            bias = []
            for d in range(WINDOW_BLOCKS):
                key = column_ids - d * rows
                seen = (key <= row) & (key.astype(jnp.float32) >= first)
                bias.append(jnp.where(seen, 0.0, -jnp.inf))

            for half in range(2):
                inner = pl.ds(half * HEAD_SIZE, HEAD_SIZE)
                kv_cols = pl.ds(pl.multiple_of(j * PAIR + half * HEAD_SIZE, HEAD_SIZE), HEAD_SIZE)
                keys = [k_own[:, kv_cols]] + [k_in[s, j, :, inner] for s in range(3)]
                values = [v_own[:, kv_cols]] + [v_in[s, j, :, inner] for s in range(3)]
                starts = [(half * HEADS_PER_GROUP + h) * HEAD_SIZE for h in range(HEADS_PER_GROUP)]
                cols = [pl.ds(pl.multiple_of(j * CHUNK + at_, HEAD_SIZE), HEAD_SIZE) for at_ in starts]
                query = jnp.concatenate([q[here, c] for c in cols], axis=0)
                scores = []
                for d in range(WINDOW_BLOCKS):
                    score = lax.dot_general(query, keys[d], NT, preferred_element_type=jnp.float32)
                    score = score.reshape(HEADS_PER_GROUP, tile, rows) + bias[d][None]
                    scores.append(score.reshape(HEADS_PER_GROUP * tile, rows))
                top = functools.reduce(jnp.maximum, scores)
                top = jnp.max(top, axis=1, keepdims=True)
                weights = [jnp.exp2((score - top) * factor) for score in scores]
                total = jnp.sum(functools.reduce(jnp.add, weights), axis=1, keepdims=True)
                mixed = functools.reduce(
                    jnp.add,
                    [
                        jnp.dot(w.astype(jnp.bfloat16), v, preferred_element_type=jnp.float32)
                        for w, v in zip(weights, values)
                    ],
                )
                attended = (mixed / total).astype(jnp.bfloat16)
                for h in range(HEADS_PER_GROUP):
                    mine = attended[h * tile : (h + 1) * tile]
                    att[here, cols[h]] = mine
                    stream = res[here, cols[h]].astype(jnp.float32) + mine.astype(jnp.float32)
                    square[t] += stream * stream
                    s_all[t, j, 1, :, pl.ds(starts[h], HEAD_SIZE)] = (
                        stream * gain_ref[:, cols[h]]
                    ).astype(jnp.bfloat16)

            @pl.when(t == 0)
            def _():
                send_rows(t, j)

            @pl.when(j == pairs - 1)
            def _():
                @pl.when(t > 0)
                def _():
                    for earlier in range(pairs):
                        send_rows(t, earlier)

                mean = jnp.sum(square[t], axis=1, keepdims=True) * (1.0 / width)
                rs_all[t, 1] = jnp.broadcast_to(lax.rsqrt(mean + 1e-05), rs_all.shape[2:])
                rs_copy(0, t).start()
                rs_copy(1, t).start()
                att_copy(t).start()

    for load in loads[4:]:
        load.wait()

    @each(TILES)
    def _(t):
        acc_gate[...] = jnp.zeros_like(acc_gate)
        acc_up[...] = jnp.zeros_like(acc_up)

        def add_chunk(j):
            s_arrival(2, t, j)
            s_arrival(3, t, j)
            cols = pl.ds(j * CHUNK, CHUNK)
            chunk = s_all[t, j].reshape(FFN_STEPS * tile, CHUNK)
            acc_gate[...] += lax.dot_general(chunk, gate[:, cols], NT, preferred_element_type=jnp.float32)
            acc_up[...] += lax.dot_general(chunk, up[:, cols], NT, preferred_element_type=jnp.float32)

        for j in range(pairs):
            s_arrival(0, t, j)
            s_copy(2, t, j).start()
            if j == pairs - 1:
                rs_arrival(0, t)
                rs_copy(2, t).start()
            if j > 0:
                add_chunk(j - 1)
        add_chunk(pairs - 1)

        rs_arrival(2, t)
        rs_arrival(3, t)
        scale = rs_all[t].reshape(FFN_STEPS * tile, HEAD_SIZE)[:, :1]
        gate_value = acc_gate[...] * scale
        silu = gate_value / (1.0 + jnp.exp(-gate_value))
        hidden[...] = (silu * (acc_up[...] * scale)).astype(jnp.bfloat16).reshape(hidden.shape)

        def combine(j):
            p_arrival(0, t, j)
            part[1, t, j] = (middle[j] + x_in[t, j].astype(jnp.float32)).astype(jnp.bfloat16)
            p_copy(1, t, j).start()

        even = core == 0
        for j in range(pairs):
            fed = hidden[...].reshape(FFN_STEPS * tile, hidden.shape[2])
            sums = jnp.dot(fed, down[:, pl.ds(j * CHUNK, CHUNK)], preferred_element_type=jnp.float32)
            sums = sums.reshape(FFN_STEPS, tile, CHUNK)
            middle[j] = sums[0]
            own_total[t, j] = sums[1]
            part[0, t, j] = jnp.where(even, sums[2], sums[3]).astype(jnp.bfloat16)
            p_copy(0, t, j).start()
            part[2, t, j] = jnp.where(even, sums[3], sums[2]).astype(jnp.bfloat16)
            p_copy(2, t, j).start()
            if j > 0:
                combine(j - 1)
        combine(pairs - 1)

    @each(TILES)
    def _(t):
        here = pl.ds(pl.multiple_of(t * tile, tile), tile)

        @each(pairs)
        def _(j):
            cols = pl.ds(pl.multiple_of(j * CHUNK, CHUNK), CHUNK)
            p_arrival(2, t, j)
            p_arrival(1, t, j)
            back = r_in[0, t, j].astype(jnp.float32) + r_in[1, t, j].astype(jnp.float32)
            ffn[here, cols] = (own_total[t, j] + back).astype(jnp.bfloat16)

        ffn_copy(t).start()

    for route in range(3):
        kv_each(route, lambda copy: copy.wait_send())

    @each(TILES)
    def _(t):
        @each(pairs)
        def _(j):
            for route in range(3):
                s_copy(route, t, j).wait_send()
                p_copy(route, t, j).wait_send()

        for route in range(3):
            rs_copy(route, t).wait_send()
        att_copy(t).wait()
        ffn_copy(t).wait()


def per_device(count, q, k, v, positions, residual, gain, gate, up, down):
    rows, width = q.shape
    units = gate.shape[0]
    tile = rows // TILES
    pairs = KEY_VALUE_HEADS // 2
    bf16, f32 = jnp.bfloat16, jnp.float32
    any_spec = pl.BlockSpec(memory_space=pl.ANY)
    vmem_spec = pl.BlockSpec(memory_space=pltpu.VMEM)
    dma = pltpu.SemaphoreType.DMA
    return pl.pallas_call(
        functools.partial(layer_kernel, count),
        out_shape=(jax.ShapeDtypeStruct((rows, width), bf16),) * 2,
        in_specs=[any_spec, any_spec, any_spec, vmem_spec, any_spec, vmem_spec] + [any_spec] * 3,
        out_specs=(any_spec, any_spec),
        scratch_shapes=[
            pltpu.VMEM((rows, width), bf16),
            pltpu.VMEM(k.shape, bf16),
            pltpu.VMEM(v.shape, bf16),
            pltpu.VMEM((rows, width), bf16),
            pltpu.VMEM((units, width), bf16),
            pltpu.VMEM((units, width), bf16),
            pltpu.VMEM((units, width), bf16),
            pltpu.VMEM((3, pairs, rows, PAIR), bf16),
            pltpu.VMEM((3, pairs, rows, PAIR), bf16),
            pltpu.VMEM((TILES, pairs, FFN_STEPS, tile, CHUNK), bf16),
            pltpu.VMEM((rows, 1), f32),
            pltpu.VMEM((TILES, tile, HEAD_SIZE), f32),
            pltpu.VMEM((TILES, FFN_STEPS, tile, HEAD_SIZE), f32),
            pltpu.VMEM((FFN_STEPS * tile, units), f32),
            pltpu.VMEM((FFN_STEPS * tile, units), f32),
            pltpu.VMEM((FFN_STEPS, tile, units), bf16),
            pltpu.VMEM((pairs, tile, CHUNK), f32),
            pltpu.VMEM((TILES, pairs, tile, CHUNK), f32),
            pltpu.VMEM((3, TILES, pairs, tile, CHUNK), bf16),
            pltpu.VMEM((TILES, pairs, tile, CHUNK), bf16),
            pltpu.VMEM((2, TILES, pairs, tile, CHUNK), bf16),
            pltpu.VMEM((rows, width), bf16),
            pltpu.VMEM((rows, width), bf16),
            dma((7,)),
            dma((TILES,)),
            dma((TILES,)),
            dma((2, 3, pairs)),
            dma((2, 3, pairs)),
            dma((3, TILES, pairs)),
            dma((4, TILES, pairs)),
            dma((3, TILES)),
            dma((4, TILES)),
            dma((3, TILES, pairs)),
            dma((3, TILES, pairs)),
        ],
        compiler_params=pltpu.CompilerParams(
            collective_id=0, has_side_effects=True, vmem_limit_bytes=60 * 2**20
        ),
    )(q, k, v, positions.reshape(1, rows), residual, gain.reshape(1, width), gate, up, down)


def solution(mesh):
    split = P("blk", None)
    in_specs = (split, split, split, P("blk"), split, P(), split, split, split)
    return jax.shard_map(
        functools.partial(per_device, mesh.shape["blk"]),
        mesh=mesh,
        in_specs=in_specs,
        out_specs=(split, split),
        check_vma=False,
    )
```

```python
import functools
import math

import jax
import jax.numpy as jnp
from jax import lax
from jax.experimental import pallas as pl
from jax.experimental.pallas import tpu as pltpu
from jax.sharding import PartitionSpec as P

HEAD_SIZE = 128
KEY_VALUE_HEADS = 8
HEADS_PER_GROUP = 4
WINDOW_BLOCKS = 4
FFN_STEPS = 4
PAIR = 2 * HEAD_SIZE
CHUNK = HEADS_PER_GROUP * PAIR
TILES = 4
MESH = pl.DeviceIdType.MESH
NT = (((1,), (1,)), ((), ()))


def layer_kernel(
    count,
    q_hbm,
    k_hbm,
    v_hbm,
    pos_ref,
    res_hbm,
    gain_ref,
    gate_hbm,
    up_hbm,
    down_hbm,
    attended_hbm,
    ffn_hbm,
    q,
    k_own,
    v_own,
    res,
    gate,
    up,
    down,
    k_in,
    v_in,
    s_all,
    first_key,
    square,
    rs_all,
    acc_gate,
    acc_up,
    hidden,
    middle,
    own_total,
    part,
    x_in,
    r_in,
    att,
    ffn,
    load_sem,
    att_sem,
    ffn_sem,
    kv_send,
    kv_recv,
    s_send,
    s_recv,
    rs_send,
    rs_recv,
    p_send,
    p_recv,
):
    rows, width = q.shape
    pairs = KEY_VALUE_HEADS // 2
    tile = rows // TILES
    me = lax.axis_index("blk")
    core = lax.rem(me, 2)

    def at(offset):
        return lax.rem(me + offset + count, count)

    third, sibling = at(1 + 2 * core), at(1 - 2 * core)
    routes = ((at(2), 1, 0), (third, 2 * core, 2 + core), (sibling, 2 - 2 * core, 3 - core))

    loads = [
        pltpu.make_async_copy(src, dst, load_sem.at[i])
        for i, (src, dst) in enumerate(
            (
                (k_hbm, k_own),
                (v_hbm, v_own),
                (q_hbm, q),
                (res_hbm, res),
                (gate_hbm, gate),
                (up_hbm, up),
                (down_hbm, down),
            )
        )
    ]
    for load in loads:
        load.start()

    barrier = pltpu.get_barrier_semaphore()
    for offset in (1, 2, 3, -1, -2, -3):
        pl.semaphore_signal(barrier, inc=1, device_id=(at(offset),), device_id_type=MESH)
    pl.semaphore_wait(barrier, 6)

    def kv_copy(which, route, j):
        device, slot, _ = routes[route]
        own, arrived = ((k_hbm, k_in), (v_hbm, v_in))[which]
        if route == 2:
            src = arrived.at[1, j]
        else:
            src = own.at[:, pl.ds(pl.multiple_of(j * PAIR, PAIR), PAIR)]
        return pltpu.make_async_remote_copy(
            src_ref=src,
            dst_ref=arrived.at[slot, j],
            send_sem=kv_send.at[which, route, j],
            recv_sem=kv_recv.at[which, slot, j],
            device_id=(device,),
            device_id_type=MESH,
        )

    def kv_arrival(which, slot, j):
        arrived = (k_in, v_in)[which]
        pltpu.make_async_copy(arrived.at[slot, j], arrived.at[slot, j], kv_recv.at[which, slot, j]).wait()

    def s_copy(route, t, j):
        device, _, place = routes[route]
        return pltpu.make_async_remote_copy(
            src_ref=s_all.at[t, j, 0 if route == 2 else 1],
            dst_ref=s_all.at[t, j, place],
            send_sem=s_send.at[route, t, j],
            recv_sem=s_recv.at[place, t, j],
            device_id=(device,),
            device_id_type=MESH,
        )

    def s_arrival(place, t, j):
        here = s_all.at[t, j, place]
        pltpu.make_async_copy(here, here, s_recv.at[place, t, j]).wait()

    def rs_copy(route, t):
        device, _, place = routes[route]
        return pltpu.make_async_remote_copy(
            src_ref=rs_all.at[t, 0 if route == 2 else 1],
            dst_ref=rs_all.at[t, place],
            send_sem=rs_send.at[route, t],
            recv_sem=rs_recv.at[place, t],
            device_id=(device,),
            device_id_type=MESH,
        )

    def rs_arrival(place, t):
        here = rs_all.at[t, place]
        pltpu.make_async_copy(here, here, rs_recv.at[place, t]).wait()

    def p_landing(kind, t, j):
        return x_in.at[t, j] if kind == 0 else r_in.at[kind - 1, t, j]

    def p_copy(kind, t, j):
        return pltpu.make_async_remote_copy(
            src_ref=part.at[kind, t, j],
            dst_ref=p_landing(kind, t, j),
            send_sem=p_send.at[kind, t, j],
            recv_sem=p_recv.at[kind, t, j],
            device_id=((sibling, at(-2), at(2 * core - 3))[kind],),
            device_id_type=MESH,
        )

    def p_arrival(kind, t, j):
        here = p_landing(kind, t, j)
        pltpu.make_async_copy(here, here, p_recv.at[kind, t, j]).wait()

    def each(limit):
        def run(body):
            lax.fori_loop(0, limit, lambda i, c: (body(i), c)[1], 0)

        return run

    sends = (me + 2 < count, me + 1 + 2 * core < count)
    reaches = (me >= 1, me >= 2, me >= 3)
    forwards = reaches[1]

    def kv_each(route, act):
        @pl.when(forwards if route == 2 else sends[route])
        def _():
            @each(pairs)
            def _(j):
                for which in range(2):
                    act(kv_copy(which, route, j))

    for route in range(2):
        kv_each(route, lambda copy: copy.start())
    for slot in range(WINDOW_BLOCKS - 1):
        @pl.when(jnp.logical_not(reaches[slot]))
        def _():
            k_in[slot] = jnp.zeros(k_in.shape[1:], k_in.dtype)
            v_in[slot] = jnp.zeros(v_in.shape[1:], v_in.dtype)

    for load in loads[:4]:
        load.wait()

    factor = math.log2(math.e) / math.sqrt(HEAD_SIZE)
    row_ids = lax.broadcasted_iota(jnp.int32, (tile, rows), 0)
    column_ids = lax.broadcasted_iota(jnp.int32, (tile, rows), 1)

    def att_copy(t):
        here = pl.ds(pl.multiple_of(t * tile, tile), tile)
        return pltpu.make_async_copy(att.at[here], attended_hbm.at[here], att_sem.at[t])

    def ffn_copy(t):
        here = pl.ds(pl.multiple_of(t * tile, tile), tile)
        return pltpu.make_async_copy(ffn.at[here], ffn_hbm.at[here], ffn_sem.at[t])

    diagonal = lax.broadcasted_iota(jnp.int32, (rows, rows), 0) - lax.broadcasted_iota(
        jnp.int32, (rows, rows), 1
    )
    back = jnp.where(diagonal == 0, pos_ref[...].astype(jnp.float32), 0.0)
    first_key[...] = (
        lax.broadcasted_iota(jnp.int32, (rows, 1), 0).astype(jnp.float32)
        - jnp.sum(back, axis=1, keepdims=True)
    )
    square[...] = jnp.zeros_like(square)

    def send_rows(t, j):
        s_copy(0, t, j).start()
        s_copy(1, t, j).start()

    def attend(t, first_tile=False):
        here = pl.ds(pl.multiple_of(t * tile, tile), tile)
        row = row_ids + t * tile
        first = first_key[here]
        bias = []
        for d in range(WINDOW_BLOCKS):
            key = column_ids - d * rows
            seen = (key <= row) & (key.astype(jnp.float32) >= first)
            bias.append(jnp.where(seen, 0.0, -jnp.inf))


        @each(pairs)
        def _(j):
            if first_tile:
                @pl.when(reaches[1])
                def _():
                    for which in range(2):
                        kv_arrival(which, 1, j)
                        kv_copy(which, 2, j).start()

                for slot in (0, 2):
                    @pl.when(reaches[slot])
                    def _():
                        for which in range(2):
                            kv_arrival(which, slot, j)

            for half in range(2):
                inner = pl.ds(half * HEAD_SIZE, HEAD_SIZE)
                kv_cols = pl.ds(pl.multiple_of(j * PAIR + half * HEAD_SIZE, HEAD_SIZE), HEAD_SIZE)
                keys = [k_own[:, kv_cols]] + [k_in[s, j, :, inner] for s in range(3)]
                values = [v_own[:, kv_cols]] + [v_in[s, j, :, inner] for s in range(3)]
                starts = [(half * HEADS_PER_GROUP + h) * HEAD_SIZE for h in range(HEADS_PER_GROUP)]
                cols = [pl.ds(pl.multiple_of(j * CHUNK + at_, HEAD_SIZE), HEAD_SIZE) for at_ in starts]
                query = jnp.concatenate([q[here, c] for c in cols], axis=0)
                scores = []
                for d in range(WINDOW_BLOCKS):
                    score = lax.dot_general(query, keys[d], NT, preferred_element_type=jnp.float32)
                    score = score.reshape(HEADS_PER_GROUP, tile, rows) + bias[d][None]
                    scores.append(score.reshape(HEADS_PER_GROUP * tile, rows))
                top = functools.reduce(jnp.maximum, scores)
                top = jnp.max(top, axis=1, keepdims=True)
                weights = [jnp.exp2((score - top) * factor) for score in scores]
                total = jnp.sum(functools.reduce(jnp.add, weights), axis=1, keepdims=True)
                mixed = functools.reduce(
                    jnp.add,
                    [
                        jnp.dot(w.astype(jnp.bfloat16), v, preferred_element_type=jnp.float32)
                        for w, v in zip(weights, values)
                    ],
                )
                attended = (mixed / total).astype(jnp.bfloat16)
                for h in range(HEADS_PER_GROUP):
                    mine = attended[h * tile : (h + 1) * tile]
                    att[here, cols[h]] = mine
                    stream = res[here, cols[h]].astype(jnp.float32) + mine.astype(jnp.float32)
                    square[t] += stream * stream
                    s_all[t, j, 1, :, pl.ds(starts[h], HEAD_SIZE)] = (
                        stream * gain_ref[:, cols[h]]
                    ).astype(jnp.bfloat16)
            send_rows(t, j)

        mean = jnp.sum(square[t], axis=1, keepdims=True) * (1.0 / width)
        rs_all[t, 1] = jnp.broadcast_to(lax.rsqrt(mean + 1e-05), rs_all.shape[2:])
        rs_copy(0, t).start()
        rs_copy(1, t).start()
        att_copy(t).start()

    attend(0, first_tile=True)
    for load in loads[4:]:
        load.wait()

    @each(TILES)
    def _(t):
        @pl.when(t + 1 < TILES)
        def _():
            attend(t + 1)

        acc_gate[...] = jnp.zeros_like(acc_gate)
        acc_up[...] = jnp.zeros_like(acc_up)

        def add_chunk(j):
            s_arrival(2, t, j)
            s_arrival(3, t, j)
            cols = pl.ds(j * CHUNK, CHUNK)
            chunk = s_all[t, j].reshape(FFN_STEPS * tile, CHUNK)
            acc_gate[...] += lax.dot_general(chunk, gate[:, cols], NT, preferred_element_type=jnp.float32)
            acc_up[...] += lax.dot_general(chunk, up[:, cols], NT, preferred_element_type=jnp.float32)

        for j in range(pairs):
            s_arrival(0, t, j)
            s_copy(2, t, j).start()
            if j == pairs - 1:
                rs_arrival(0, t)
                rs_copy(2, t).start()
            if j > 0:
                add_chunk(j - 1)
        add_chunk(pairs - 1)

        rs_arrival(2, t)
        rs_arrival(3, t)
        scale = rs_all[t].reshape(FFN_STEPS * tile, HEAD_SIZE)[:, :1]
        gate_value = acc_gate[...] * scale
        silu = gate_value / (1.0 + jnp.exp(-gate_value))
        hidden[...] = (silu * (acc_up[...] * scale)).astype(jnp.bfloat16).reshape(hidden.shape)

        def combine(j):
            p_arrival(0, t, j)
            part[1, t, j] = (middle[j] + x_in[t, j].astype(jnp.float32)).astype(jnp.bfloat16)
            p_copy(1, t, j).start()

        even = core == 0
        for j in range(pairs):
            fed = hidden[...].reshape(FFN_STEPS * tile, hidden.shape[2])
            sums = jnp.dot(fed, down[:, pl.ds(j * CHUNK, CHUNK)], preferred_element_type=jnp.float32)
            sums = sums.reshape(FFN_STEPS, tile, CHUNK)
            middle[j] = sums[0]
            own_total[t, j] = sums[1]
            part[0, t, j] = jnp.where(even, sums[2], sums[3]).astype(jnp.bfloat16)
            p_copy(0, t, j).start()
            part[2, t, j] = jnp.where(even, sums[3], sums[2]).astype(jnp.bfloat16)
            p_copy(2, t, j).start()
            if j > 0:
                combine(j - 1)
        combine(pairs - 1)

    @each(TILES)
    def _(t):
        here = pl.ds(pl.multiple_of(t * tile, tile), tile)

        @each(pairs)
        def _(j):
            cols = pl.ds(pl.multiple_of(j * CHUNK, CHUNK), CHUNK)
            p_arrival(2, t, j)
            p_arrival(1, t, j)
            back = r_in[0, t, j].astype(jnp.float32) + r_in[1, t, j].astype(jnp.float32)
            ffn[here, cols] = (own_total[t, j] + back).astype(jnp.bfloat16)

        ffn_copy(t).start()

    for route in range(3):
        kv_each(route, lambda copy: copy.wait_send())

    @each(TILES)
    def _(t):
        @each(pairs)
        def _(j):
            for route in range(3):
                s_copy(route, t, j).wait_send()
                p_copy(route, t, j).wait_send()

        for route in range(3):
            rs_copy(route, t).wait_send()
        att_copy(t).wait()
        ffn_copy(t).wait()


def per_device(count, q, k, v, positions, residual, gain, gate, up, down):
    rows, width = q.shape
    units = gate.shape[0]
    tile = rows // TILES
    pairs = KEY_VALUE_HEADS // 2
    bf16, f32 = jnp.bfloat16, jnp.float32
    any_spec = pl.BlockSpec(memory_space=pl.ANY)
    vmem_spec = pl.BlockSpec(memory_space=pltpu.VMEM)
    dma = pltpu.SemaphoreType.DMA
    return pl.pallas_call(
        functools.partial(layer_kernel, count),
        out_shape=(jax.ShapeDtypeStruct((rows, width), bf16),) * 2,
        in_specs=[any_spec, any_spec, any_spec, vmem_spec, any_spec, vmem_spec] + [any_spec] * 3,
        out_specs=(any_spec, any_spec),
        scratch_shapes=[
            pltpu.VMEM((rows, width), bf16),
            pltpu.VMEM(k.shape, bf16),
            pltpu.VMEM(v.shape, bf16),
            pltpu.VMEM((rows, width), bf16),
            pltpu.VMEM((units, width), bf16),
            pltpu.VMEM((units, width), bf16),
            pltpu.VMEM((units, width), bf16),
            pltpu.VMEM((3, pairs, rows, PAIR), bf16),
            pltpu.VMEM((3, pairs, rows, PAIR), bf16),
            pltpu.VMEM((TILES, pairs, FFN_STEPS, tile, CHUNK), bf16),
            pltpu.VMEM((rows, 1), f32),
            pltpu.VMEM((TILES, tile, HEAD_SIZE), f32),
            pltpu.VMEM((TILES, FFN_STEPS, tile, HEAD_SIZE), f32),
            pltpu.VMEM((FFN_STEPS * tile, units), f32),
            pltpu.VMEM((FFN_STEPS * tile, units), f32),
            pltpu.VMEM((FFN_STEPS, tile, units), bf16),
            pltpu.VMEM((pairs, tile, CHUNK), f32),
            pltpu.VMEM((TILES, pairs, tile, CHUNK), f32),
            pltpu.VMEM((3, TILES, pairs, tile, CHUNK), bf16),
            pltpu.VMEM((TILES, pairs, tile, CHUNK), bf16),
            pltpu.VMEM((2, TILES, pairs, tile, CHUNK), bf16),
            pltpu.VMEM((rows, width), bf16),
            pltpu.VMEM((rows, width), bf16),
            dma((7,)),
            dma((TILES,)),
            dma((TILES,)),
            dma((2, 3, pairs)),
            dma((2, 3, pairs)),
            dma((3, TILES, pairs)),
            dma((4, TILES, pairs)),
            dma((3, TILES)),
            dma((4, TILES)),
            dma((3, TILES, pairs)),
            dma((3, TILES, pairs)),
        ],
        compiler_params=pltpu.CompilerParams(
            collective_id=0, has_side_effects=True, vmem_limit_bytes=60 * 2**20
        ),
    )(q, k, v, positions.reshape(1, rows), residual, gain.reshape(1, width), gate, up, down)


def solution(mesh):
    split = P("blk", None)
    in_specs = (split, split, split, P("blk"), split, P(), split, split, split)
    return jax.shard_map(
        functools.partial(per_device, mesh.shape["blk"]),
        mesh=mesh,
        in_specs=in_specs,
        out_specs=(split, split),
        check_vma=False,
    )
```

```python
import functools
import math

import jax
import jax.numpy as jnp
from jax import lax
from jax.experimental import pallas as pl
from jax.experimental.pallas import tpu as pltpu
from jax.sharding import PartitionSpec as P

HEAD_SIZE = 128
KEY_VALUE_HEADS = 8
HEADS_PER_GROUP = 4
WINDOW_BLOCKS = 4
FFN_STEPS = 4
PAIR = 2 * HEAD_SIZE
CHUNK = HEADS_PER_GROUP * PAIR
TILES = 4
MESH = pl.DeviceIdType.MESH
NT = (((1,), (1,)), ((), ()))


def layer_kernel(
    count,
    q_hbm,
    k_hbm,
    v_hbm,
    pos_ref,
    res_hbm,
    gain_ref,
    gate_hbm,
    up_hbm,
    down_hbm,
    attended_hbm,
    ffn_hbm,
    q,
    k_own,
    v_own,
    res,
    gate,
    up,
    down,
    k_in,
    v_in,
    s_all,
    first_key,
    square,
    rs_all,
    acc_gate,
    acc_up,
    hidden,
    middle,
    own_total,
    part,
    x_in,
    r_in,
    att,
    ffn,
    load_sem,
    att_sem,
    ffn_sem,
    kv_send,
    kv_recv,
    s_send,
    s_recv,
    rs_send,
    rs_recv,
    p_send,
    p_recv,
):
    rows, width = q.shape
    pairs = KEY_VALUE_HEADS // 2
    tile = rows // TILES
    me = lax.axis_index("blk")
    core = lax.rem(me, 2)

    def at(offset):
        return lax.rem(me + offset + count, count)

    third, sibling = at(1 + 2 * core), at(1 - 2 * core)
    odd_chip = lax.rem(lax.div(me, 2), 2) == 1
    direct = jnp.logical_not(odd_chip & (core == 1))
    relay = odd_chip & (core == 0)
    routes = (
        (at(2), 1, 0),
        (third, 2 * core, 2 + core),
        (sibling, 2 - 2 * core, 3 - core),
        (at(-1), 1, 0),
    )
    source_place = (1, 1, 0, 3)

    loads = [
        pltpu.make_async_copy(src, dst, load_sem.at[i])
        for i, (src, dst) in enumerate(
            (
                (k_hbm, k_own),
                (v_hbm, v_own),
                (q_hbm, q),
                (res_hbm, res),
                (gate_hbm, gate),
                (up_hbm, up),
                (down_hbm, down),
            )
        )
    ]
    for load in loads:
        load.start()

    barrier = pltpu.get_barrier_semaphore()
    for offset in (1, 2, 3, -1, -2, -3):
        pl.semaphore_signal(barrier, inc=1, device_id=(at(offset),), device_id_type=MESH)
    pl.semaphore_wait(barrier, 6)

    def kv_copy(which, route, j):
        device, slot, _ = routes[route]
        own, arrived = ((k_hbm, k_in), (v_hbm, v_in))[which]
        if route >= 2:
            src = arrived.at[route - 1, j]
        else:
            src = own.at[:, pl.ds(pl.multiple_of(j * PAIR, PAIR), PAIR)]
        return pltpu.make_async_remote_copy(
            src_ref=src,
            dst_ref=arrived.at[slot, j],
            send_sem=kv_send.at[which, route, j],
            recv_sem=kv_recv.at[which, slot, j],
            device_id=(device,),
            device_id_type=MESH,
        )

    def kv_arrival(which, slot, j):
        arrived = (k_in, v_in)[which]
        pltpu.make_async_copy(arrived.at[slot, j], arrived.at[slot, j], kv_recv.at[which, slot, j]).wait()

    def s_copy(route, t, j):
        device, _, place = routes[route]
        return pltpu.make_async_remote_copy(
            src_ref=s_all.at[t, j, source_place[route]],
            dst_ref=s_all.at[t, j, place],
            send_sem=s_send.at[route, t, j],
            recv_sem=s_recv.at[place, t, j],
            device_id=(device,),
            device_id_type=MESH,
        )

    def s_arrival(place, t, j):
        here = s_all.at[t, j, place]
        pltpu.make_async_copy(here, here, s_recv.at[place, t, j]).wait()

    def rs_copy(route, t):
        device, _, place = routes[route]
        return pltpu.make_async_remote_copy(
            src_ref=rs_all.at[t, source_place[route]],
            dst_ref=rs_all.at[t, place],
            send_sem=rs_send.at[route, t],
            recv_sem=rs_recv.at[place, t],
            device_id=(device,),
            device_id_type=MESH,
        )

    def rs_arrival(place, t):
        here = rs_all.at[t, place]
        pltpu.make_async_copy(here, here, rs_recv.at[place, t]).wait()

    def p_landing(kind, t, j):
        return x_in.at[t, j] if kind == 0 else r_in.at[kind - 1, t, j]

    def p_copy(kind, t, j):
        return pltpu.make_async_remote_copy(
            src_ref=part.at[kind, t, j],
            dst_ref=p_landing(kind, t, j),
            send_sem=p_send.at[kind, t, j],
            recv_sem=p_recv.at[kind, t, j],
            device_id=((sibling, at(-2), at(2 * core - 3))[kind],),
            device_id_type=MESH,
        )

    def p_arrival(kind, t, j):
        here = p_landing(kind, t, j)
        pltpu.make_async_copy(here, here, p_recv.at[kind, t, j]).wait()

    def each(limit):
        def run(body):
            lax.fori_loop(0, limit, lambda i, c: (body(i), c)[1], 0)

        return run

    reaches = (me >= 1, me >= 2, me >= 3)
    sends = (
        direct & (me + 2 < count),
        me + 1 + 2 * core < count,
        reaches[1],
        relay & reaches[2],
    )

    def kv_each(route, act):
        @pl.when(sends[route])
        def _():
            @each(pairs)
            def _(j):
                for which in range(2):
                    act(kv_copy(which, route, j))

    for route in range(2):
        kv_each(route, lambda copy: copy.start())
    for slot in range(WINDOW_BLOCKS - 1):
        @pl.when(jnp.logical_not(reaches[slot]))
        def _():
            k_in[slot] = jnp.zeros(k_in.shape[1:], k_in.dtype)
            v_in[slot] = jnp.zeros(v_in.shape[1:], v_in.dtype)

    for load in loads[:4]:
        load.wait()

    factor = math.log2(math.e) / math.sqrt(HEAD_SIZE)
    row_ids = lax.broadcasted_iota(jnp.int32, (tile, rows), 0)
    column_ids = lax.broadcasted_iota(jnp.int32, (tile, rows), 1)

    def att_copy(t):
        here = pl.ds(pl.multiple_of(t * tile, tile), tile)
        return pltpu.make_async_copy(att.at[here], attended_hbm.at[here], att_sem.at[t])

    def ffn_copy(t):
        here = pl.ds(pl.multiple_of(t * tile, tile), tile)
        return pltpu.make_async_copy(ffn.at[here], ffn_hbm.at[here], ffn_sem.at[t])

    diagonal = lax.broadcasted_iota(jnp.int32, (rows, rows), 0) - lax.broadcasted_iota(
        jnp.int32, (rows, rows), 1
    )
    back = jnp.where(diagonal == 0, pos_ref[...].astype(jnp.float32), 0.0)
    first_key[...] = (
        lax.broadcasted_iota(jnp.int32, (rows, 1), 0).astype(jnp.float32)
        - jnp.sum(back, axis=1, keepdims=True)
    )
    square[...] = jnp.zeros_like(square)

    def send_rows(t, j):
        @pl.when(direct)
        def _():
            s_copy(0, t, j).start()

        s_copy(1, t, j).start()

    def attend(t, first_tile=False):
        here = pl.ds(pl.multiple_of(t * tile, tile), tile)
        row = row_ids + t * tile
        first = first_key[here]
        bias = []
        for d in range(WINDOW_BLOCKS):
            key = column_ids - d * rows
            seen = (key <= row) & (key.astype(jnp.float32) >= first)
            bias.append(jnp.where(seen, 0.0, -jnp.inf))


        @each(pairs)
        def _(j):
            if first_tile:
                @pl.when(reaches[2])
                def _():
                    @pl.when(relay)
                    def _():
                        for which in range(2):
                            kv_arrival(which, 2, j)
                            kv_copy(which, 3, j).start()

                @pl.when(reaches[1])
                def _():
                    for which in range(2):
                        kv_arrival(which, 1, j)
                        kv_copy(which, 2, j).start()

                for slot, waits in ((0, reaches[0]), (2, reaches[2] & jnp.logical_not(relay))):
                    @pl.when(waits)
                    def _():
                        for which in range(2):
                            kv_arrival(which, slot, j)

            for half in range(2):
                inner = pl.ds(half * HEAD_SIZE, HEAD_SIZE)
                kv_cols = pl.ds(pl.multiple_of(j * PAIR + half * HEAD_SIZE, HEAD_SIZE), HEAD_SIZE)
                keys = [k_own[:, kv_cols]] + [k_in[s, j, :, inner] for s in range(3)]
                values = [v_own[:, kv_cols]] + [v_in[s, j, :, inner] for s in range(3)]
                starts = [(half * HEADS_PER_GROUP + h) * HEAD_SIZE for h in range(HEADS_PER_GROUP)]
                cols = [pl.ds(pl.multiple_of(j * CHUNK + at_, HEAD_SIZE), HEAD_SIZE) for at_ in starts]
                query = jnp.concatenate([q[here, c] for c in cols], axis=0)
                scores = []
                for d in range(WINDOW_BLOCKS):
                    score = lax.dot_general(query, keys[d], NT, preferred_element_type=jnp.float32)
                    score = score.reshape(HEADS_PER_GROUP, tile, rows) + bias[d][None]
                    scores.append(score.reshape(HEADS_PER_GROUP * tile, rows))
                top = functools.reduce(jnp.maximum, scores)
                top = jnp.max(top, axis=1, keepdims=True)
                weights = [jnp.exp2((score - top) * factor) for score in scores]
                total = jnp.sum(functools.reduce(jnp.add, weights), axis=1, keepdims=True)
                mixed = functools.reduce(
                    jnp.add,
                    [
                        jnp.dot(w.astype(jnp.bfloat16), v, preferred_element_type=jnp.float32)
                        for w, v in zip(weights, values)
                    ],
                )
                attended = (mixed / total).astype(jnp.bfloat16)
                for h in range(HEADS_PER_GROUP):
                    mine = attended[h * tile : (h + 1) * tile]
                    att[here, cols[h]] = mine
                    stream = res[here, cols[h]].astype(jnp.float32) + mine.astype(jnp.float32)
                    square[t] += stream * stream
                    s_all[t, j, 1, :, pl.ds(starts[h], HEAD_SIZE)] = (
                        stream * gain_ref[:, cols[h]]
                    ).astype(jnp.bfloat16)
            send_rows(t, j)

        mean = jnp.sum(square[t], axis=1, keepdims=True) * (1.0 / width)
        rs_all[t, 1] = jnp.broadcast_to(lax.rsqrt(mean + 1e-05), rs_all.shape[2:])
        @pl.when(direct)
        def _():
            rs_copy(0, t).start()

        rs_copy(1, t).start()
        att_copy(t).start()

    attend(0, first_tile=True)
    for load in loads[4:]:
        load.wait()

    @each(TILES)
    def _(t):
        @pl.when(t + 1 < TILES)
        def _():
            attend(t + 1)

        acc_gate[...] = jnp.zeros_like(acc_gate)
        acc_up[...] = jnp.zeros_like(acc_up)

        def add_chunk(j):
            s_arrival(2, t, j)

            @pl.when(jnp.logical_not(relay))
            def _():
                s_arrival(3, t, j)

            cols = pl.ds(j * CHUNK, CHUNK)
            chunk = s_all[t, j].reshape(FFN_STEPS * tile, CHUNK)
            acc_gate[...] += lax.dot_general(chunk, gate[:, cols], NT, preferred_element_type=jnp.float32)
            acc_up[...] += lax.dot_general(chunk, up[:, cols], NT, preferred_element_type=jnp.float32)

        for j in range(pairs):
            @pl.when(relay)
            def _():
                s_arrival(3, t, j)
                s_copy(3, t, j).start()
                if j == pairs - 1:
                    rs_arrival(3, t)
                    rs_copy(3, t).start()

            s_arrival(0, t, j)
            s_copy(2, t, j).start()
            if j == pairs - 1:
                rs_arrival(0, t)
                rs_copy(2, t).start()
            if j > 0:
                add_chunk(j - 1)
        add_chunk(pairs - 1)

        rs_arrival(2, t)

        @pl.when(jnp.logical_not(relay))
        def _():
            rs_arrival(3, t)

        scale = rs_all[t].reshape(FFN_STEPS * tile, HEAD_SIZE)[:, :1]
        gate_value = acc_gate[...] * scale
        silu = gate_value / (1.0 + jnp.exp(-gate_value))
        hidden[...] = (silu * (acc_up[...] * scale)).astype(jnp.bfloat16).reshape(hidden.shape)

        def combine(j):
            p_arrival(0, t, j)
            part[1, t, j] = (middle[j] + x_in[t, j].astype(jnp.float32)).astype(jnp.bfloat16)
            p_copy(1, t, j).start()

        even = core == 0
        for j in range(pairs):
            fed = hidden[...].reshape(FFN_STEPS * tile, hidden.shape[2])
            sums = jnp.dot(fed, down[:, pl.ds(j * CHUNK, CHUNK)], preferred_element_type=jnp.float32)
            sums = sums.reshape(FFN_STEPS, tile, CHUNK)
            middle[j] = sums[0]
            own_total[t, j] = sums[1]
            part[0, t, j] = jnp.where(even, sums[2], sums[3]).astype(jnp.bfloat16)
            p_copy(0, t, j).start()
            part[2, t, j] = jnp.where(even, sums[3], sums[2]).astype(jnp.bfloat16)
            p_copy(2, t, j).start()
            if j > 0:
                combine(j - 1)
        combine(pairs - 1)

    @each(TILES)
    def _(t):
        here = pl.ds(pl.multiple_of(t * tile, tile), tile)

        @each(pairs)
        def _(j):
            cols = pl.ds(pl.multiple_of(j * CHUNK, CHUNK), CHUNK)
            p_arrival(2, t, j)
            p_arrival(1, t, j)
            back = r_in[0, t, j].astype(jnp.float32) + r_in[1, t, j].astype(jnp.float32)
            ffn[here, cols] = (own_total[t, j] + back).astype(jnp.bfloat16)

        ffn_copy(t).start()

    for route in range(4):
        kv_each(route, lambda copy: copy.wait_send())

    @each(TILES)
    def _(t):
        for route, started in ((0, direct), (1, None), (2, None), (3, relay)):
            def finish(route=route):
                rs_copy(route, t).wait_send()

                @each(pairs)
                def _(j):
                    s_copy(route, t, j).wait_send()

            if started is None:
                finish()
            else:
                pl.when(started)(finish)

        @each(pairs)
        def _(j):
            for kind in range(3):
                p_copy(kind, t, j).wait_send()

        att_copy(t).wait()
        ffn_copy(t).wait()


def per_device(count, q, k, v, positions, residual, gain, gate, up, down):
    rows, width = q.shape
    units = gate.shape[0]
    tile = rows // TILES
    pairs = KEY_VALUE_HEADS // 2
    bf16, f32 = jnp.bfloat16, jnp.float32
    any_spec = pl.BlockSpec(memory_space=pl.ANY)
    vmem_spec = pl.BlockSpec(memory_space=pltpu.VMEM)
    dma = pltpu.SemaphoreType.DMA
    return pl.pallas_call(
        functools.partial(layer_kernel, count),
        out_shape=(jax.ShapeDtypeStruct((rows, width), bf16),) * 2,
        in_specs=[any_spec, any_spec, any_spec, vmem_spec, any_spec, vmem_spec] + [any_spec] * 3,
        out_specs=(any_spec, any_spec),
        scratch_shapes=[
            pltpu.VMEM((rows, width), bf16),
            pltpu.VMEM(k.shape, bf16),
            pltpu.VMEM(v.shape, bf16),
            pltpu.VMEM((rows, width), bf16),
            pltpu.VMEM((units, width), bf16),
            pltpu.VMEM((units, width), bf16),
            pltpu.VMEM((units, width), bf16),
            pltpu.VMEM((3, pairs, rows, PAIR), bf16),
            pltpu.VMEM((3, pairs, rows, PAIR), bf16),
            pltpu.VMEM((TILES, pairs, FFN_STEPS, tile, CHUNK), bf16),
            pltpu.VMEM((rows, 1), f32),
            pltpu.VMEM((TILES, tile, HEAD_SIZE), f32),
            pltpu.VMEM((TILES, FFN_STEPS, tile, HEAD_SIZE), f32),
            pltpu.VMEM((FFN_STEPS * tile, units), f32),
            pltpu.VMEM((FFN_STEPS * tile, units), f32),
            pltpu.VMEM((FFN_STEPS, tile, units), bf16),
            pltpu.VMEM((pairs, tile, CHUNK), f32),
            pltpu.VMEM((TILES, pairs, tile, CHUNK), f32),
            pltpu.VMEM((3, TILES, pairs, tile, CHUNK), bf16),
            pltpu.VMEM((TILES, pairs, tile, CHUNK), bf16),
            pltpu.VMEM((2, TILES, pairs, tile, CHUNK), bf16),
            pltpu.VMEM((rows, width), bf16),
            pltpu.VMEM((rows, width), bf16),
            dma((7,)),
            dma((TILES,)),
            dma((TILES,)),
            dma((2, 4, pairs)),
            dma((2, 3, pairs)),
            dma((4, TILES, pairs)),
            dma((4, TILES, pairs)),
            dma((4, TILES)),
            dma((4, TILES)),
            dma((3, TILES, pairs)),
            dma((3, TILES, pairs)),
        ],
        compiler_params=pltpu.CompilerParams(
            collective_id=0, has_side_effects=True, vmem_limit_bytes=60 * 2**20
        ),
    )(q, k, v, positions.reshape(1, rows), residual, gain.reshape(1, width), gate, up, down)


def solution(mesh):
    split = P("blk", None)
    in_specs = (split, split, split, P("blk"), split, P(), split, split, split)
    return jax.shard_map(
        functools.partial(per_device, mesh.shape["blk"]),
        mesh=mesh,
        in_specs=in_specs,
        out_specs=(split, split),
        check_vma=False,
    )
```

```python
import functools
import math

import jax
import jax.numpy as jnp
from jax import lax
from jax.experimental import pallas as pl
from jax.experimental.pallas import tpu as pltpu
from jax.sharding import PartitionSpec as P

HEAD_SIZE = 128
KEY_VALUE_HEADS = 8
HEADS_PER_GROUP = 4
WINDOW_BLOCKS = 4
FFN_STEPS = 4
PAIR = 2 * HEAD_SIZE
CHUNK = HEADS_PER_GROUP * PAIR
TILES = 4
MESH = pl.DeviceIdType.MESH
NT = (((1,), (1,)), ((), ()))


def layer_kernel(
    count,
    q_hbm,
    k_hbm,
    v_hbm,
    pos_ref,
    res_hbm,
    gain_ref,
    gate_hbm,
    up_hbm,
    down_hbm,
    attended_hbm,
    ffn_hbm,
    q,
    k_own,
    v_own,
    res,
    gate,
    up,
    down,
    k_in,
    v_in,
    s_all,
    first_key,
    square,
    rs_all,
    acc_gate,
    acc_up,
    hidden,
    middle,
    own_total,
    part,
    x_in,
    y_in,
    late,
    r_in,
    att,
    ffn,
    load_sem,
    att_sem,
    ffn_sem,
    kv_send,
    kv_recv,
    s_send,
    s_recv,
    rs_send,
    rs_recv,
    p_send,
    p_recv,
):
    rows, width = q.shape
    pairs = KEY_VALUE_HEADS // 2
    tile = rows // TILES
    me = lax.axis_index("blk")
    core = lax.rem(me, 2)

    def at(offset):
        return lax.rem(me + offset + count, count)

    third, sibling = at(1 + 2 * core), at(1 - 2 * core)
    odd_chip = lax.rem(lax.div(me, 2), 2) == 1
    direct = jnp.logical_not(odd_chip & (core == 1))
    relay = odd_chip & (core == 0)
    hands_on = jnp.logical_not(odd_chip) & (core == 1)
    routes = (
        (at(2), 1, 0),
        (third, 2 * core, 2 + core),
        (sibling, 2 - 2 * core, 3 - core),
        (at(-1), 1, 0),
    )
    source_place = (1, 1, 0, 3)

    loads = [
        pltpu.make_async_copy(src, dst, load_sem.at[i])
        for i, (src, dst) in enumerate(
            (
                (k_hbm, k_own),
                (v_hbm, v_own),
                (q_hbm, q),
                (res_hbm, res),
                (gate_hbm, gate),
                (up_hbm, up),
                (down_hbm, down),
            )
        )
    ]
    for load in loads:
        load.start()

    barrier = pltpu.get_barrier_semaphore()
    for offset in (1, 2, 3, -1, -2, -3):
        pl.semaphore_signal(barrier, inc=1, device_id=(at(offset),), device_id_type=MESH)
    pl.semaphore_wait(barrier, 6)

    def kv_copy(which, route, j):
        device, slot, _ = routes[route]
        own, arrived = ((k_hbm, k_in), (v_hbm, v_in))[which]
        if route >= 2:
            src = arrived.at[route - 1, j]
        else:
            src = own.at[:, pl.ds(pl.multiple_of(j * PAIR, PAIR), PAIR)]
        return pltpu.make_async_remote_copy(
            src_ref=src,
            dst_ref=arrived.at[slot, j],
            send_sem=kv_send.at[which, route, j],
            recv_sem=kv_recv.at[which, slot, j],
            device_id=(device,),
            device_id_type=MESH,
        )

    def kv_arrival(which, slot, j):
        arrived = (k_in, v_in)[which]
        pltpu.make_async_copy(arrived.at[slot, j], arrived.at[slot, j], kv_recv.at[which, slot, j]).wait()

    def s_copy(route, t, j):
        device, _, place = routes[route]
        return pltpu.make_async_remote_copy(
            src_ref=s_all.at[t, j, source_place[route]],
            dst_ref=s_all.at[t, j, place],
            send_sem=s_send.at[route, t, j],
            recv_sem=s_recv.at[place, t, j],
            device_id=(device,),
            device_id_type=MESH,
        )

    def s_arrival(place, t, j):
        here = s_all.at[t, j, place]
        pltpu.make_async_copy(here, here, s_recv.at[place, t, j]).wait()

    def rs_copy(route, t):
        device, _, place = routes[route]
        return pltpu.make_async_remote_copy(
            src_ref=rs_all.at[t, source_place[route]],
            dst_ref=rs_all.at[t, place],
            send_sem=rs_send.at[route, t],
            recv_sem=rs_recv.at[place, t],
            device_id=(device,),
            device_id_type=MESH,
        )

    def rs_arrival(place, t):
        here = rs_all.at[t, place]
        pltpu.make_async_copy(here, here, rs_recv.at[place, t]).wait()

    def p_landing(kind, t, j):
        if kind == 3:
            return y_in.at[t, j]
        return x_in.at[t, j] if kind == 0 else r_in.at[kind - 1, t, j]

    def p_copy(kind, t, j):
        return pltpu.make_async_remote_copy(
            src_ref=part.at[1 if kind == 3 else kind, t, j],
            dst_ref=p_landing(kind, t, j),
            send_sem=p_send.at[kind, t, j],
            recv_sem=p_recv.at[kind, t, j],
            device_id=((sibling, at(-2), at(2 * core - 3), at(1))[kind],),
            device_id_type=MESH,
        )

    def p_arrival(kind, t, j):
        here = p_landing(kind, t, j)
        pltpu.make_async_copy(here, here, p_recv.at[kind, t, j]).wait()

    def each(limit):
        def run(body):
            lax.fori_loop(0, limit, lambda i, c: (body(i), c)[1], 0)

        return run

    reaches = (me >= 1, me >= 2, me >= 3)
    sends = (
        direct & (me + 2 < count),
        me + 1 + 2 * core < count,
        reaches[1],
        relay & reaches[2],
    )

    def kv_each(route, act):
        @pl.when(sends[route])
        def _():
            @each(pairs)
            def _(j):
                for which in range(2):
                    act(kv_copy(which, route, j))

    for route in range(2):
        kv_each(route, lambda copy: copy.start())
    for slot in range(WINDOW_BLOCKS - 1):
        @pl.when(jnp.logical_not(reaches[slot]))
        def _():
            k_in[slot] = jnp.zeros(k_in.shape[1:], k_in.dtype)
            v_in[slot] = jnp.zeros(v_in.shape[1:], v_in.dtype)

    for load in loads[:4]:
        load.wait()

    factor = math.log2(math.e) / math.sqrt(HEAD_SIZE)
    row_ids = lax.broadcasted_iota(jnp.int32, (tile, rows), 0)
    column_ids = lax.broadcasted_iota(jnp.int32, (tile, rows), 1)

    def att_copy(t):
        here = pl.ds(pl.multiple_of(t * tile, tile), tile)
        return pltpu.make_async_copy(att.at[here], attended_hbm.at[here], att_sem.at[t])

    def ffn_copy(t):
        here = pl.ds(pl.multiple_of(t * tile, tile), tile)
        return pltpu.make_async_copy(ffn.at[here], ffn_hbm.at[here], ffn_sem.at[t])

    diagonal = lax.broadcasted_iota(jnp.int32, (rows, rows), 0) - lax.broadcasted_iota(
        jnp.int32, (rows, rows), 1
    )
    back = jnp.where(diagonal == 0, pos_ref[...].astype(jnp.float32), 0.0)
    first_key[...] = (
        lax.broadcasted_iota(jnp.int32, (rows, 1), 0).astype(jnp.float32)
        - jnp.sum(back, axis=1, keepdims=True)
    )
    square[...] = jnp.zeros_like(square)

    def send_rows(t, j):
        @pl.when(direct)
        def _():
            s_copy(0, t, j).start()

        s_copy(1, t, j).start()

    def attend(t, first_tile=False):
        here = pl.ds(pl.multiple_of(t * tile, tile), tile)
        row = row_ids + t * tile
        first = first_key[here]
        bias = []
        for d in range(WINDOW_BLOCKS):
            key = column_ids - d * rows
            seen = (key <= row) & (key.astype(jnp.float32) >= first)
            bias.append(jnp.where(seen, 0.0, -jnp.inf))


        @each(pairs)
        def _(j):
            if first_tile:
                @pl.when(reaches[2])
                def _():
                    @pl.when(relay)
                    def _():
                        for which in range(2):
                            kv_arrival(which, 2, j)
                            kv_copy(which, 3, j).start()

                @pl.when(reaches[1])
                def _():
                    for which in range(2):
                        kv_arrival(which, 1, j)
                        kv_copy(which, 2, j).start()

                for slot, waits in ((0, reaches[0]), (2, reaches[2] & jnp.logical_not(relay))):
                    @pl.when(waits)
                    def _():
                        for which in range(2):
                            kv_arrival(which, slot, j)

            for half in range(2):
                inner = pl.ds(half * HEAD_SIZE, HEAD_SIZE)
                kv_cols = pl.ds(pl.multiple_of(j * PAIR + half * HEAD_SIZE, HEAD_SIZE), HEAD_SIZE)
                keys = [k_own[:, kv_cols]] + [k_in[s, j, :, inner] for s in range(3)]
                values = [v_own[:, kv_cols]] + [v_in[s, j, :, inner] for s in range(3)]
                starts = [(half * HEADS_PER_GROUP + h) * HEAD_SIZE for h in range(HEADS_PER_GROUP)]
                cols = [pl.ds(pl.multiple_of(j * CHUNK + at_, HEAD_SIZE), HEAD_SIZE) for at_ in starts]
                query = jnp.concatenate([q[here, c] for c in cols], axis=0)
                scores = []
                for d in range(WINDOW_BLOCKS):
                    score = lax.dot_general(query, keys[d], NT, preferred_element_type=jnp.float32)
                    score = score.reshape(HEADS_PER_GROUP, tile, rows) + bias[d][None]
                    scores.append(score.reshape(HEADS_PER_GROUP * tile, rows))
                top = functools.reduce(jnp.maximum, scores)
                top = jnp.max(top, axis=1, keepdims=True)
                weights = [jnp.exp2((score - top) * factor) for score in scores]
                total = jnp.sum(functools.reduce(jnp.add, weights), axis=1, keepdims=True)
                mixed = functools.reduce(
                    jnp.add,
                    [
                        jnp.dot(w.astype(jnp.bfloat16), v, preferred_element_type=jnp.float32)
                        for w, v in zip(weights, values)
                    ],
                )
                attended = (mixed / total).astype(jnp.bfloat16)
                for h in range(HEADS_PER_GROUP):
                    mine = attended[h * tile : (h + 1) * tile]
                    att[here, cols[h]] = mine
                    stream = res[here, cols[h]].astype(jnp.float32) + mine.astype(jnp.float32)
                    square[t] += stream * stream
                    s_all[t, j, 1, :, pl.ds(starts[h], HEAD_SIZE)] = (
                        stream * gain_ref[:, cols[h]]
                    ).astype(jnp.bfloat16)
            send_rows(t, j)

        mean = jnp.sum(square[t], axis=1, keepdims=True) * (1.0 / width)
        rs_all[t, 1] = jnp.broadcast_to(lax.rsqrt(mean + 1e-05), rs_all.shape[2:])
        @pl.when(direct)
        def _():
            rs_copy(0, t).start()

        rs_copy(1, t).start()
        att_copy(t).start()

    attend(0, first_tile=True)
    for load in loads[4:]:
        load.wait()

    @each(TILES)
    def _(t):
        @pl.when(t + 1 < TILES)
        def _():
            attend(t + 1)

        acc_gate[...] = jnp.zeros_like(acc_gate)
        acc_up[...] = jnp.zeros_like(acc_up)

        def add_chunk(j):
            s_arrival(2, t, j)

            @pl.when(jnp.logical_not(relay))
            def _():
                s_arrival(3, t, j)

            cols = pl.ds(j * CHUNK, CHUNK)
            chunk = s_all[t, j].reshape(FFN_STEPS * tile, CHUNK)
            acc_gate[...] += lax.dot_general(chunk, gate[:, cols], NT, preferred_element_type=jnp.float32)
            acc_up[...] += lax.dot_general(chunk, up[:, cols], NT, preferred_element_type=jnp.float32)

        for j in range(pairs):
            @pl.when(relay)
            def _():
                s_arrival(3, t, j)
                s_copy(3, t, j).start()
                if j == pairs - 1:
                    rs_arrival(3, t)
                    rs_copy(3, t).start()

            s_arrival(0, t, j)
            s_copy(2, t, j).start()
            if j == pairs - 1:
                rs_arrival(0, t)
                rs_copy(2, t).start()
            if j > 0:
                add_chunk(j - 1)
        add_chunk(pairs - 1)

        rs_arrival(2, t)

        @pl.when(jnp.logical_not(relay))
        def _():
            rs_arrival(3, t)

        scale = rs_all[t].reshape(FFN_STEPS * tile, HEAD_SIZE)[:, :1]
        gate_value = acc_gate[...] * scale
        silu = gate_value / (1.0 + jnp.exp(-gate_value))
        hidden[...] = (silu * (acc_up[...] * scale)).astype(jnp.bfloat16).reshape(hidden.shape)

        def combine(j):
            p_arrival(0, t, j)
            part[1, t, j] = (middle[j] + x_in[t, j].astype(jnp.float32)).astype(jnp.bfloat16)

            @pl.when(hands_on)
            def _():
                p_copy(3, t, j).start()

            @pl.when(jnp.logical_not(hands_on))
            def _():
                p_copy(1, t, j).start()

        even = core == 0
        for j in range(pairs):
            fed = hidden[...].reshape(FFN_STEPS * tile, hidden.shape[2])
            sums = jnp.dot(fed, down[:, pl.ds(j * CHUNK, CHUNK)], preferred_element_type=jnp.float32)
            sums = sums.reshape(FFN_STEPS, tile, CHUNK)
            middle[j] = sums[0]
            own_total[t, j] = sums[1]
            part[0, t, j] = jnp.where(even, sums[2], sums[3]).astype(jnp.bfloat16)
            p_copy(0, t, j).start()
            late[j] = jnp.where(even, sums[3], sums[2])

            @pl.when(jnp.logical_not(relay))
            def _():
                part[2, t, j] = late[j].astype(jnp.bfloat16)
                p_copy(2, t, j).start()

            if j > 0:
                combine(j - 1)
        combine(pairs - 1)

        @pl.when(relay)
        def _():
            @each(pairs)
            def _(j):
                p_arrival(3, t, j)
                part[2, t, j] = (late[j] + y_in[t, j].astype(jnp.float32)).astype(jnp.bfloat16)
                p_copy(2, t, j).start()

    @each(TILES)
    def _(t):
        here = pl.ds(pl.multiple_of(t * tile, tile), tile)

        @each(pairs)
        def _(j):
            cols = pl.ds(pl.multiple_of(j * CHUNK, CHUNK), CHUNK)
            p_arrival(2, t, j)
            own_total[t, j] += r_in[1, t, j].astype(jnp.float32)

            @pl.when(direct)
            def _():
                p_arrival(1, t, j)
                own_total[t, j] += r_in[0, t, j].astype(jnp.float32)

            ffn[here, cols] = own_total[t, j].astype(jnp.bfloat16)

        ffn_copy(t).start()

    for route in range(4):
        kv_each(route, lambda copy: copy.wait_send())

    @each(TILES)
    def _(t):
        for route, started in ((0, direct), (1, None), (2, None), (3, relay)):
            def finish(route=route):
                rs_copy(route, t).wait_send()

                @each(pairs)
                def _(j):
                    s_copy(route, t, j).wait_send()

            if started is None:
                finish()
            else:
                pl.when(started)(finish)

        @each(pairs)
        def _(j):
            p_copy(0, t, j).wait_send()
            p_copy(2, t, j).wait_send()

            @pl.when(hands_on)
            def _():
                p_copy(3, t, j).wait_send()

            @pl.when(jnp.logical_not(hands_on))
            def _():
                p_copy(1, t, j).wait_send()

        att_copy(t).wait()
        ffn_copy(t).wait()


def per_device(count, q, k, v, positions, residual, gain, gate, up, down):
    rows, width = q.shape
    units = gate.shape[0]
    tile = rows // TILES
    pairs = KEY_VALUE_HEADS // 2
    bf16, f32 = jnp.bfloat16, jnp.float32
    any_spec = pl.BlockSpec(memory_space=pl.ANY)
    vmem_spec = pl.BlockSpec(memory_space=pltpu.VMEM)
    dma = pltpu.SemaphoreType.DMA
    return pl.pallas_call(
        functools.partial(layer_kernel, count),
        out_shape=(jax.ShapeDtypeStruct((rows, width), bf16),) * 2,
        in_specs=[any_spec, any_spec, any_spec, vmem_spec, any_spec, vmem_spec] + [any_spec] * 3,
        out_specs=(any_spec, any_spec),
        scratch_shapes=[
            pltpu.VMEM((rows, width), bf16),
            pltpu.VMEM(k.shape, bf16),
            pltpu.VMEM(v.shape, bf16),
            pltpu.VMEM((rows, width), bf16),
            pltpu.VMEM((units, width), bf16),
            pltpu.VMEM((units, width), bf16),
            pltpu.VMEM((units, width), bf16),
            pltpu.VMEM((3, pairs, rows, PAIR), bf16),
            pltpu.VMEM((3, pairs, rows, PAIR), bf16),
            pltpu.VMEM((TILES, pairs, FFN_STEPS, tile, CHUNK), bf16),
            pltpu.VMEM((rows, 1), f32),
            pltpu.VMEM((TILES, tile, HEAD_SIZE), f32),
            pltpu.VMEM((TILES, FFN_STEPS, tile, HEAD_SIZE), f32),
            pltpu.VMEM((FFN_STEPS * tile, units), f32),
            pltpu.VMEM((FFN_STEPS * tile, units), f32),
            pltpu.VMEM((FFN_STEPS, tile, units), bf16),
            pltpu.VMEM((pairs, tile, CHUNK), f32),
            pltpu.VMEM((TILES, pairs, tile, CHUNK), f32),
            pltpu.VMEM((3, TILES, pairs, tile, CHUNK), bf16),
            pltpu.VMEM((TILES, pairs, tile, CHUNK), bf16),
            pltpu.VMEM((TILES, pairs, tile, CHUNK), bf16),
            pltpu.VMEM((pairs, tile, CHUNK), f32),
            pltpu.VMEM((2, TILES, pairs, tile, CHUNK), bf16),
            pltpu.VMEM((rows, width), bf16),
            pltpu.VMEM((rows, width), bf16),
            dma((7,)),
            dma((TILES,)),
            dma((TILES,)),
            dma((2, 4, pairs)),
            dma((2, 3, pairs)),
            dma((4, TILES, pairs)),
            dma((4, TILES, pairs)),
            dma((4, TILES)),
            dma((4, TILES)),
            dma((4, TILES, pairs)),
            dma((4, TILES, pairs)),
        ],
        compiler_params=pltpu.CompilerParams(
            collective_id=0, has_side_effects=True, vmem_limit_bytes=60 * 2**20
        ),
    )(q, k, v, positions.reshape(1, rows), residual, gain.reshape(1, width), gate, up, down)


def solution(mesh):
    split = P("blk", None)
    in_specs = (split, split, split, P("blk"), split, P(), split, split, split)
    return jax.shard_map(
        functools.partial(per_device, mesh.shape["blk"]),
        mesh=mesh,
        in_specs=in_specs,
        out_specs=(split, split),
        check_vma=False,
    )
```
